512 devices in a mesh: px: 16 (over y, core), py: 32 (over z, x).
Axes of the slice: x: 4, y: 8, z: 8, core: 2. Of those that a mesh axis runs over, the one named last changes fastest.
Arguments:
- right_side: float32 [16, 32, 16512], P('px', 'py')
- geometry: float32 [16, 32, 3, 48, 512], P('px', 'py'), may hold values from 0.3 to 3
- shift: float32 [16, 32, 48], P('px', 'py'), may hold values from 4 to 40
- node_order: int32 [16, 32, 48, 512], P('px', 'py'), may hold values from 0 to 511, as said below
- elem_counts: int32 [16, 32], P('px', 'py'), may hold values from 18 to 48, as said below
- share_lists: int32 [16, 32, 4, 1536], P('px', 'py'), may hold values from 0 to 1280, as said below
Outputs:
- solution_field: float32 [16, 32, 16512], P('px', 'py')
- residual: float32 [16, 32, 16512], P('px', 'py')
The draws below stay inside these ranges and needn't reach their ends.
Inputs may be any that keep to these rules, and one draw needn't show every extreme that they name: Every row node_order[i, j, e, :] is a permutation of 0 to 511. `elem_counts`: some partition has exactly 48 live elements. `share_lists`: the used entries of each part of a list come first and are distinct; the k-th used face entry of a partition's list toward a neighbour and of the neighbour's list back name the same node, and the k-th node of a crossing is the same node in the four partitions around it, in every list that names that crossing. Partitions at the grid's ends have no used entries toward missing neighbours. Some face has 1280 shared nodes and some crossing 128.
All inputs are finite; a program needn't handle non-finite values.
Results may differ from the reference program's by a relative error of at most 0.0003.
Values sent between devices are 32-bit elements; how exact they have to be, the bound alone decides.
A program may use at most 64 MiB of HBM per device.

```python
import math
import jax
import jax.numpy as jnp
import numpy as np
from jax import lax

ELEM_DEV = 48
NODES = 512
STRIDE = 344
ITERS = 2
LOC = 16512
FACE = 1280
DIAG = 128
N_PX = 16
N_PY = 32


def distinct_order(key, shape):
    scores = jax.random.randint(key, shape, 0, 2 ** 16)
    ranked = scores * 16384 + lax.broadcasted_iota(jnp.int32, shape, len(shape) - 1)
    return jnp.argsort(ranked, axis=-1).astype(jnp.int32)


def forced_counts(key, rows_count, cols_count, lowest, highest):
    first, second = jax.random.split(key)
    counts_drawn = jax.random.randint(first, (rows_count, cols_count), lowest, highest + 1)
    chosen = jax.random.randint(second, (), 0, rows_count * cols_count)
    ranking = jnp.arange(rows_count * cols_count).reshape(rows_count, cols_count)
    return jnp.where(ranking == chosen, highest, counts_drawn).astype(jnp.int32)


def draw_right_side(key, part):
    key = jax.random.fold_in(key, 11)
    ranking = (jnp.arange(N_PX)[:, None] * N_PY + jnp.arange(N_PY)[None, :]).astype(jnp.float32)
    growth = 4.0 * 3.0 ** (ranking / (N_PX * N_PY - 1))
    values_drawn = jax.random.normal(key, (N_PX, N_PY, LOC), jnp.float32)
    return (values_drawn * growth[:, :, None]).astype(jnp.float32)


def draw_node_order(key, part):
    key = jax.random.fold_in(key, 5)
    return distinct_order(key, (N_PX, N_PY, ELEM_DEV, NODES)).astype(jnp.int32)


def draw_elem_counts(key, part):
    key = jax.random.fold_in(key, 7)
    return forced_counts(key, N_PX, N_PY, ELEM_DEV * 3 // 8, ELEM_DEV)


def draw_share_lists(key, part):
    key = jax.random.fold_in(key, 9)
    pieces = jax.random.split(key, 5)
    along_x = jnp.pad(forced_counts(pieces[0], N_PX - 1, N_PY, FACE // 2, FACE), ((0, 1), (0, 0)))
    along_y = jnp.pad(forced_counts(pieces[1], N_PX, N_PY - 1, FACE // 2, FACE), ((0, 0), (0, 1)))
    crossing = jnp.pad(forced_counts(pieces[2], N_PX - 1, N_PY - 1, DIAG // 2, DIAG), ((1, 1), (1, 1)))
    below_x = jnp.pad(along_x, ((1, 0), (0, 0)))[:N_PX]
    before_y = jnp.pad(along_y, ((0, 0), (1, 0)))[:, :N_PY]

    def corner(step_rows, step_cols):
        return crossing[step_rows:step_rows + N_PX, step_cols:step_cols + N_PY]
    face_counts = jnp.stack([along_x, below_x, along_y, before_y], axis=2)
    lower_counts = jnp.stack([corner(1, 0), corner(0, 0), corner(0, 1), corner(0, 0)], axis=2)
    upper_counts = jnp.stack([corner(1, 1), corner(0, 1), corner(1, 1), corner(1, 0)], axis=2)
    face_order = distinct_order(pieces[3], (N_PX, N_PY, 4, FACE))
    corner_order = distinct_order(pieces[4], (N_PX, N_PY, 4, DIAG))
    lower_order = corner_order[:, :, jnp.array([1, 3, 2, 3])]
    upper_order = corner_order[:, :, jnp.array([0, 2, 0, 1])]
    face_slots = jnp.arange(FACE)
    corner_slots = jnp.arange(DIAG)
    face_part = jnp.where(face_slots < face_counts[..., None], face_order, FACE)
    lower_part = jnp.where(corner_slots < lower_counts[..., None], lower_order, DIAG)
    upper_part = jnp.where(corner_slots < upper_counts[..., None], upper_order, DIAG)
    return jnp.concatenate([face_part, lower_part, upper_part], axis=3).astype(jnp.int32)


def level_of(own_key, dims, cuts, least, high):
    def one(dim, parts):
        steps = jax.random.uniform(jax.random.fold_in(jax.random.fold_in(own_key, 6), dim), (parts,), jnp.float32, least / len(cuts), high / len(cuts))
        return jnp.repeat(jnp.exp(steps), dims[dim] // parts).reshape((-1,) + (1,) * (len(dims) - dim - 1))

    level = one(*cuts[0])
    for cut in cuts[1:]:
        level = level * one(*cut)
    return level


def setup_inputs(seed: int = 0) -> dict:
    arg_keys = jax.random.split(jax.random.key(seed), 7)
    return {
        "right_side": draw_right_side(jax.random.fold_in(arg_keys[6], 71), 0),
        "geometry": jnp.clip(jnp.exp(math.log(3.0) - 2.3025851 * jax.random.uniform(arg_keys[1], (N_PX, N_PY, 3, ELEM_DEV, NODES), jnp.float32) ** level_of(arg_keys[1], (N_PX, N_PY, 3, ELEM_DEV, NODES), ((0, 16), (1, 32)), -0.2, 0.2)), 0.3, 3.0),
        "shift": jnp.clip(jnp.exp(math.log(40.0) - 2.3025851 * jax.random.uniform(arg_keys[2], (N_PX, N_PY, ELEM_DEV), jnp.float32) ** level_of(arg_keys[2], (N_PX, N_PY, ELEM_DEV), ((0, 16), (1, 32)), -0.2, 0.2)), 4.0, 40.0),
        "node_order": draw_node_order(jax.random.fold_in(arg_keys[6], 71), 0),
        "elem_counts": draw_elem_counts(jax.random.fold_in(arg_keys[6], 71), 0),
        "share_lists": draw_share_lists(jax.random.fold_in(arg_keys[6], 71), 0),
    }


def gll_derivative():
    degree = 7
    points = np.array([-1.0, -0.8717401485096066, -0.5917001814331423, -0.2092992179024789, 0.2092992179024789, 0.5917001814331423, 0.8717401485096066, 1.0])
    before = np.ones(8)
    current = points * 1.0
    for order in range(1, degree):
        following = ((2 * order + 1) * points * current - order * before) / (order + 1)
        before = current
        current = following
    legendre = current
    same = np.arange(8)[:, None] == np.arange(8)[None, :]
    spacing = np.where(same, 1.0, points[:, None] - points[None, :])
    matrix = np.where(same, 0.0, legendre[:, None] / (legendre[None, :] * spacing))
    corner = np.array([-14.0, 0.0, 0.0, 0.0, 0.0, 0.0, 0.0, 14.0])
    return matrix + np.where(same, corner[:, None], 0.0)


def direction_tables():
    deriv = gll_derivative()
    first_table = np.kron(deriv, np.eye(64))
    second_table = np.kron(np.eye(2), np.kron(deriv, np.eye(8)))
    third_table = np.kron(np.eye(16), deriv)
    return first_table, second_table, third_table


def node_index_of(order_dev, live):
    row_ids = jnp.arange(order_dev.shape[0], dtype=jnp.int32)[:, None]
    return ((row_ids * STRIDE + order_dev) % (live * STRIDE)).astype(jnp.int32)


def element_terms(values_in, node_index, geo_dev, shift_vals, alive):
    first_np, second_np, third_np = direction_tables()
    first_table = jnp.asarray(first_np, dtype=jnp.float32)
    second_table = jnp.asarray(second_np, dtype=jnp.float32)
    third_table = jnp.asarray(third_np, dtype=jnp.float32)
    exact = lax.Precision.HIGHEST
    rows = node_index.shape[0]
    gathered = jnp.take(values_in, node_index, axis=0)
    narrow = gathered.reshape(rows * 4, 128)
    grad_r = jnp.dot(gathered, first_table.T, precision=exact)
    grad_s = jnp.dot(narrow, second_table.T, precision=exact).reshape(rows, 512)
    grad_t = jnp.dot(narrow, third_table.T, precision=exact).reshape(rows, 512)
    result = jnp.dot(geo_dev[0] * grad_r, first_table, precision=exact)
    back_s = jnp.dot((geo_dev[1] * grad_s).reshape(rows * 4, 128), second_table, precision=exact)
    back_t = jnp.dot((geo_dev[2] * grad_t).reshape(rows * 4, 128), third_table, precision=exact)
    result = result + back_s.reshape(rows, 512) + back_t.reshape(rows, 512)
    result = result + shift_vals[:, None] * gathered
    return result * alive[:, None]


def rolled(grid_array, step_rows, step_cols):
    return jnp.roll(grid_array, (step_rows, step_cols), axis=(0, 1))


def reference(right_side, geometry, shift, node_order, elem_counts, share_lists):
    devices = N_PX * N_PY
    grid_rank = (jnp.arange(N_PX, dtype=jnp.int32)[:, None] * N_PY + jnp.arange(N_PY, dtype=jnp.int32)[None, :]).astype(jnp.int32)
    position = jnp.arange(LOC, dtype=jnp.int32)
    identity = (grid_rank[:, :, None] * LOC + position[None, None, :]).reshape(-1).astype(jnp.int32)
    lists = share_lists
    pp_base = 4 * FACE
    pm_base = 4 * FACE + DIAG
    mp_base = 4 * FACE + 2 * DIAG
    mm_base = 4 * FACE + 3 * DIAG
    upper_from = FACE + DIAG
    shared_kinds = [
        (lists[:, :, 1, :FACE], FACE, FACE, rolled(grid_rank, 1, 0), 0, rolled(lists[:, :, 0, :FACE], 1, 0)),
        (lists[:, :, 3, :FACE], FACE, 3 * FACE, rolled(grid_rank, 0, 1), 2 * FACE, rolled(lists[:, :, 2, :FACE], 0, 1)),
        (lists[:, :, 1, upper_from:], DIAG, mp_base, rolled(grid_rank, 1, 0), pp_base, rolled(lists[:, :, 0, upper_from:], 1, 0)),
        (lists[:, :, 3, upper_from:], DIAG, pm_base, rolled(grid_rank, 0, 1), pp_base, rolled(lists[:, :, 2, upper_from:], 0, 1)),
        (lists[:, :, 1, FACE:upper_from], DIAG, mm_base, rolled(grid_rank, 1, 1), pp_base, rolled(lists[:, :, 0, upper_from:], 1, 1)),
    ]
    for my_entries, region_size, my_base, owner_rank, owner_base, theirs in shared_kinds:
        is_valid = my_entries < region_size
        where_to = jnp.where(is_valid, grid_rank[:, :, None] * LOC + my_base + my_entries, devices * LOC).astype(jnp.int32)
        owner_id = (owner_rank[:, :, None] * LOC + owner_base + theirs).astype(jnp.int32)
        identity = identity.at[where_to.reshape(-1)].set(owner_id.reshape(-1), mode="drop")

    def assemble_all(partial_flat):
        totals = jax.ops.segment_sum(partial_flat, identity, num_segments=devices * LOC)
        return totals[identity]

    flat_geo = geometry.reshape(devices, 3, ELEM_DEV, NODES)
    flat_shift = shift.reshape(devices, ELEM_DEV)
    flat_order = node_order.reshape(devices, ELEM_DEV, NODES)
    flat_counts = elem_counts.reshape(devices)

    def one_device(packed):
        values_in, geo_dev, shift_dev, order_dev, live = packed
        node_index = node_index_of(order_dev, live)
        alive = (jnp.arange(ELEM_DEV, dtype=jnp.int32) < live).astype(jnp.float32)
        terms = element_terms(values_in, node_index, geo_dev, shift_dev, alive)
        return jnp.zeros((LOC,), jnp.float32).at[node_index.reshape(-1)].add(terms.reshape(-1))

    def operate(values_flat):
        partial_value = lax.map(one_device, (values_flat.reshape(devices, LOC), flat_geo, flat_shift, flat_order, flat_counts))
        return assemble_all(partial_value.reshape(-1))

    multiplicity = assemble_all(jnp.ones((devices * LOC,), jnp.float32))
    inverse = 1.0 / multiplicity

    def inner(first, second):
        return jnp.sum(first * second * inverse)

    live_mask = position[None, None, :] < (elem_counts[:, :, None] * STRIDE)
    rhs_live = jnp.where(live_mask, right_side, 0.0).reshape(-1)
    residual = assemble_all(rhs_live)
    solution_field = jnp.zeros_like(residual)
    direction = residual
    norm_now = inner(residual, residual)
    for step in range(ITERS):
        image = operate(direction)
        alpha = norm_now / inner(direction, image)
        solution_field = solution_field + alpha * direction
        residual = residual - alpha * image
        norm_next = inner(residual, residual)
        direction = residual + (norm_next / norm_now) * direction
        norm_now = norm_next
    return solution_field.reshape(N_PX, N_PY, LOC), residual.reshape(N_PX, N_PY, LOC)
```

```python
import functools

import jax
import jax.numpy as jnp
import numpy as np
from jax import lax
from jax.experimental import pallas as pl
from jax.experimental.pallas import tpu as pltpu
from jax.sharding import PartitionSpec as P

STRIDE = 344
FACE = 1280
DIAG = 128
ELEMS = 48
LANES = 128
ROWS = 129
PAD = 136
FACE_ROWS = FACE // LANES
TURN = 80
ROW_OF = [e * STRIDE // LANES for e in range(ELEMS)]
LOWER = (1, 3, 2, 3)
UPPER = (0, 2, 0, 1)
FACE_STEPS = ((1, 0), (-1, 0), (0, 1), (0, -1))
DIAG_STEPS = ((1, 1), (1, -1), (-1, 1), (-1, -1))
DIAG_LIST = (0, 0, 1, 1)


def gll_derivative():
    degree = 7
    points = np.array(
        [
            -1.0,
            -0.8717401485096066,
            -0.5917001814331423,
            -0.2092992179024789,
            0.2092992179024789,
            0.5917001814331423,
            0.8717401485096066,
            1.0,
        ]
    )
    before = np.ones(8)
    current = points * 1.0
    for order in range(1, degree):
        following = ((2 * order + 1) * points * current - order * before) / (order + 1)
        before = current
        current = following
    same = np.arange(8)[:, None] == np.arange(8)[None, :]
    spacing = np.where(same, 1.0, points[:, None] - points[None, :])
    matrix = np.where(same, 0.0, current[:, None] / (current[None, :] * spacing))
    corner = np.array([-14.0, 0.0, 0.0, 0.0, 0.0, 0.0, 0.0, 14.0])
    return matrix + np.where(same, corner[:, None], 0.0)


def tables():
    deriv = gll_derivative()
    half = np.arange(LANES) // 64

    def lanes_of(matrix):
        rows = []
        for out in range(4):
            for src in range(4):
                rows.append(matrix[2 * out + half, 2 * src + half])
                rows.append(matrix[2 * out + half, 2 * src + 1 - half])
        return np.stack(rows)

    coef = np.concatenate([lanes_of(deriv), lanes_of(deriv.T)])
    second = np.kron(np.eye(2), np.kron(deriv, np.eye(8)))
    third = np.kron(np.eye(16), deriv)
    ahead = np.concatenate([second.T, third.T], axis=1)
    back = np.concatenate([second, third], axis=0)
    return tuple(np.asarray(t, np.float32) for t in (coef, ahead, back))


def take_lanes(values, lanes):
    return jnp.take_along_axis(values, lanes, axis=1, mode="promise_in_bounds")


def pick(sources, index):
    high = index >> 7
    lanes = index & 127
    total = None
    for j, source in enumerate(sources):
        term = jnp.where(high == j, take_lanes(source, lanes), 0.0)
        total = term if total is None else total + term
    return total


def eight(row):
    return jnp.broadcast_to(row, (8, row.shape[1]))


def iota(shape, dim):
    return lax.broadcasted_iota(jnp.int32, shape, dim)


def one_hot_lanes(low):
    return jnp.where(low == iota((LANES, low.shape[1]), 0), 1.0, 0.0).astype(jnp.bfloat16)


def over_lanes(left, right):
    return lax.dot_general(
        left, right, (((1,), (1,)), ((), ())), preferred_element_type=jnp.float32
    )


def inverse_rows(high, low, groups):
    count = high.shape[1]
    number = iota((groups, count), 1) + 1
    hit = high == iota((groups, count), 0)
    tens = jnp.where(hit, number >> 4, 0).astype(jnp.float32)
    ones = jnp.where(hit, number & 15, 0).astype(jnp.float32)
    left = jnp.concatenate([tens, ones], axis=0).astype(jnp.bfloat16)
    found = over_lanes(left, one_hot_lanes(low))
    return (16.0 * found[:groups] + found[groups:]).astype(jnp.int32) - 1


def kernel(
    n_px,
    n_py,
    rhs_ref,
    geo_ref,
    shift_ref,
    order_ref,
    count_ref,
    lists_ref,
    coef_ref,
    ahead_ref,
    back_ref,
    sol_ref,
    res_ref,
    resid,
    image,
    second,
    part_w,
    windows,
    spread,
    sums,
    elem_inv,
    face_inv,
    cross_inv,
    wrap_inv,
    inv_mult,
    cross_src,
    send,
    recv,
    recv_diag,
    red,
    send_sem,
    recv_sem,
):
    px = lax.axis_index("px")
    py = lax.axis_index("py")

    def moved(step_x, step_y):
        return (lax.rem(px + step_x + n_px, n_px), lax.rem(py + step_y + n_py, n_py))

    low_py = 4 if n_py >= 16 else 2
    phases = (
        ((1, 2), (1, low_py)),
        ((2, n_px // 2), (1, 1)),
        ((1, 1), (low_py, n_py // low_py)),
    )

    def place(phase):
        (stride_x, size_x), (stride_y, size_y) = phase
        at_x = lax.rem(px // stride_x, size_x)
        at_y = lax.rem(py // stride_y, size_y)
        return at_x, at_y

    def partners(phase):
        (stride_x, size_x), (stride_y, size_y) = phase
        at_x, at_y = place(phase)
        found = []
        for dx in range(size_x):
            for dy in range(size_y):
                if dx or dy:
                    to_x = lax.rem(at_x + dx, size_x)
                    to_y = lax.rem(at_y + dy, size_y)
                    found.append((px + (to_x - at_x) * stride_x, py + (to_y - at_y) * stride_y))
        return found

    everyone = [moved(*step) for step in FACE_STEPS + DIAG_STEPS]
    for phase in phases:
        everyone += partners(phase)
    barrier = pltpu.get_barrier_semaphore()
    for other in everyone:
        pl.semaphore_signal(
            barrier, inc=1, device_id=other, device_id_type=pl.DeviceIdType.MESH
        )

    copies = []

    def start_copy(src, dst, other):
        number = len(copies)
        copy = pltpu.make_async_remote_copy(
            src_ref=src,
            dst_ref=dst,
            send_sem=send_sem.at[number],
            recv_sem=recv_sem.at[number],
            device_id=other,
            device_id_type=pl.DeviceIdType.MESH,
        )
        copy.start()
        copies.append(copy)
        return copy

    def start_exchange(turn):
        started = []
        for f, step in enumerate(FACE_STEPS):
            started.append(
                start_copy(
                    send.at[pl.ds(TURN * turn + 16 * f, 16)],
                    recv.at[pl.ds(TURN * turn + 16 * (f ^ 1), 16)],
                    moved(*step),
                )
            )
        for d, step in enumerate(DIAG_STEPS):
            started.append(
                start_copy(
                    send.at[pl.ds(TURN * turn + 16 * DIAG_LIST[d] + 8, 8)],
                    recv_diag.at[pl.ds(32 * turn + 8 * (3 - d), 8)],
                    moved(*step),
                )
            )
        return started

    def start_sum(turn, number, block):
        phase = phases[number]
        at_x, at_y = place(phase)
        mine = at_x * phase[1][1] + at_y
        red[turn, number, pl.ds(mine, 1)] = block[None]
        return [
            start_copy(red.at[turn, number, mine], red.at[turn, number, mine], other)
            for other in partners(phase)
        ]

    def end_sum(turn, number, started):
        for copy in started:
            copy.wait_recv()
        size = phases[number][0][1] * phases[number][1][1]
        total = red[turn, number, 0]
        for slot in range(1, size):
            total = total + red[turn, number, slot]
        return total

    live = count_ref[...]

    def fill_send(turn, source):
        for i in range(FACE_ROWS):
            index = lists_ref[:, i * LANES : (i + 1) * LANES]
            found = pick(
                [source[pl.ds(j, 4, stride=FACE_ROWS), :] for j in range(FACE_ROWS)], index
            )
            send[pl.ds(TURN * turn + i, 4, stride=16), :] = found
        first = 4 * FACE_ROWS
        for part, regions in enumerate((LOWER, UPPER)):
            for f, q in enumerate(regions):
                cross_src[4 * part + f : 4 * part + f + 1, :] = source[first + q : first + q + 1, :]
        for part in range(2):
            at = FACE + part * DIAG
            found = pick(
                [cross_src[4 * part : 4 * part + 4, :]], lists_ref[:, at : at + DIAG]
            )
            send[pl.ds(TURN * turn + FACE_ROWS + part, 4, stride=16), :] = found

    def add_received(turn, target):
        def sent_row(i):
            return recv[pl.ds(TURN * turn + i, 4, stride=16), :]

        def diagonal_row(q, i):
            at = 32 * turn + 8 * q + i
            return recv_diag[at : at + 1, :]

        for i in range(FACE_ROWS):
            index = face_inv[pl.ds(i, 4, stride=16), :]
            found = pick([sent_row(j) for j in range(FACE_ROWS)], index)
            target[pl.ds(i, 4, stride=FACE_ROWS), :] += found
        blank = jnp.zeros((2, LANES), jnp.float32)
        lower = sent_row(FACE_ROWS) + jnp.concatenate(
            [blank, diagonal_row(2, 2), diagonal_row(3, 3)], axis=0
        )
        upper = sent_row(FACE_ROWS + 1) + jnp.concatenate(
            [blank, diagonal_row(0, 2), diagonal_row(1, 3)], axis=0
        )
        lower = pick([lower], cross_inv[0:4, :])
        upper = pick([upper], cross_inv[4:8, :])
        first = 4 * FACE_ROWS
        for part, regions in ((lower, LOWER), (upper, UPPER)):
            for f, q in enumerate(regions):
                target[first + q : first + q + 1, :] += part[f : f + 1]

    element = iota((ELEMS, LANES), 0)
    offset = (element * STRIDE) & 127
    is_last = element == live - 1

    def orders(c):
        return order_ref[:, c * LANES : (c + 1) * LANES]

    def last_row(values):
        return jnp.sum(jnp.where(is_last, values, jnp.zeros_like(values)), axis=0, keepdims=True)

    def set_up():
        for f in range(4):
            row = lists_ref[f : f + 1, 0:FACE]
            face_inv[16 * f : 16 * f + 16, :] = inverse_rows(row >> 7, row & 127, 16)
            for part in range(2):
                at = FACE + part * DIAG
                row = lists_ref[f : f + 1, at : at + DIAG]
                number = (iota((8, DIAG), 1) + 1).astype(jnp.float32).astype(jnp.bfloat16)
                found = over_lanes(number, one_hot_lanes(row))
                cross_inv[4 * part + f : 4 * part + f + 1, :] = found[0:1].astype(jnp.int32) - 1
        inv_mult[...] = jnp.ones_like(inv_mult)
        for f in range(4):
            named = face_inv[16 * f : 16 * f + FACE_ROWS, :] >= 0
            inv_mult[f * FACE_ROWS : (f + 1) * FACE_ROWS, :] = jnp.where(named, 0.5, 1.0)
        for q in range(4):
            copies_of = jnp.ones((1, LANES), jnp.float32)
            for part, regions in enumerate((LOWER, UPPER)):
                for f, region in enumerate(regions):
                    if region == q:
                        row = cross_inv[4 * part + f : 4 * part + f + 1, :]
                        copies_of = copies_of + jnp.where(row >= 0, 1.5, 0.0)
            at = 4 * FACE_ROWS + q
            inv_mult[at : at + 1, :] = 1.0 / copies_of

        @pl.loop(0, ELEMS // 8)
        def _(group):
            block = order_ref[pl.ds(pl.multiple_of(8 * group, 8), 8), :]
            for s in range(8):
                e = 8 * group + s
                row = block[s : s + 1]
                shifted = row + lax.rem(e * STRIDE, LANES)
                own = jnp.where(live <= e, 0, jnp.where(live == e + 1, STRIDE, 4 * LANES))
                high = jnp.where(row >= own, 7, shifted >> 7)
                elem_inv[pl.ds(pl.multiple_of(8 * e, 8), 8), :] = inverse_rows(
                    high, shifted & 127, 8
                )

        wrapped = jnp.concatenate([last_row(orders(c)) for c in range(4)], axis=1) - STRIDE
        wrap_inv[...] = inverse_rows(wrapped >> 7, wrapped & 127, 8)

    def derivative(chunks, first):
        swapped = [pltpu.roll(u, 64, 1) for u in chunks]
        result = []
        for out in range(4):
            total = None
            for src in range(4):
                at = first + (out * 4 + src) * 2
                term = coef_ref[at : at + 1, :] * chunks[src]
                total = term if total is None else total + term
                total = total + coef_ref[at + 1 : at + 2, :] * swapped[src]
            result.append(total)
        return result

    def stacked(k):
        return jnp.concatenate(
            [geo_ref[k, :, c * LANES : (c + 1) * LANES] for c in range(4)], axis=0
        )

    def operate(source):
        for e, row in enumerate(ROW_OF):
            windows[8 * e : 8 * e + 8, :] = source[row : row + 8, :]
        rows = [windows[pl.ds(k, ELEMS, stride=8), :] for k in range(5)]
        chunks = []
        for c in range(4):
            order = orders(c)
            around = pick(
                [eight(source[0:1, :]), eight(source[1:2, :])], eight(last_row(order)) - STRIDE
            )[0:1]
            values = pick(rows, order + offset)
            chunks.append(jnp.where(is_last & (order >= STRIDE), around, values))
        exact = lax.Precision.HIGHEST
        narrow = jnp.concatenate(chunks, axis=0)
        grads = jnp.dot(
            narrow, ahead_ref[...], precision=exact, preferred_element_type=jnp.float32
        )
        fluxes = jnp.concatenate(
            [stacked(1) * grads[:, :LANES], stacked(2) * grads[:, LANES:]], axis=1
        )
        terms = jnp.dot(
            fluxes, back_ref[...], precision=exact, preferred_element_type=jnp.float32
        )
        grad = derivative(chunks, 0)
        grad = [geo_ref[0, :, c * LANES : (c + 1) * LANES] * grad[c] for c in range(4)]
        first = derivative(grad, 32)
        factor = shift_ref[...]
        result = [
            terms[c * ELEMS : (c + 1) * ELEMS] + first[c] + factor * chunks[c] for c in range(4)
        ]
        for k in range(5):
            spread[pl.ds(k, ELEMS, stride=8), :] = pick(
                result, elem_inv[pl.ds(k, ELEMS, stride=8), :]
            )
        for e, row in enumerate(ROW_OF):
            sums[e % 3, row : row + 8, :] = spread[8 * e : 8 * e + 8, :]
        sums[0, 0:8, :] += pick([eight(last_row(r)) for r in result], wrap_inv[...])
        return sums[0] + sums[1] + sums[2]

    def dots(*products):
        rows = [jnp.sum(p, axis=0, keepdims=True) for p in products]
        rows.append(jnp.zeros((8 - len(rows), LANES), jnp.float32))
        return jnp.concatenate(rows, axis=0)

    send[...] = jnp.zeros_like(send)
    spread[...] = jnp.zeros_like(spread)
    sums[...] = jnp.zeros_like(sums)
    resid[...] = jnp.zeros_like(resid)
    slot = iota((ROWS, LANES), 0) * LANES + iota((ROWS, LANES), 1)
    resid[0:ROWS, :] = jnp.where(slot < live * STRIDE, rhs_ref[...], 0.0)
    fill_send(0, resid)
    pl.semaphore_wait(barrier, len(everyone))
    exchange = start_exchange(0)
    set_up()
    for copy in exchange:
        copy.wait_recv()
    add_received(0, resid)

    part_w[...] = operate(resid)
    image[...] = part_w[...]
    fill_send(1, image)
    exchange = start_exchange(1)
    res0 = resid[...]
    summing = start_sum(0, 0, dots(res0 * res0 * inv_mult[...], res0 * part_w[...]))
    for copy in exchange:
        copy.wait_recv()
    add_received(1, image)
    summing = start_sum(0, 1, end_sum(0, 0, summing))

    second[...] = operate(image)
    fill_send(2, second)
    exchange = start_exchange(2)
    summing = start_sum(0, 2, end_sum(0, 1, summing))
    totals = jnp.sum(end_sum(0, 2, summing), axis=1, keepdims=True)
    norm0 = totals[0:1]
    energy0 = totals[1:2]
    alpha0 = norm0 / energy0

    res0 = resid[...]
    image0 = image[...]
    res1 = res0 - alpha0 * image0
    scaled = res1 * inv_mult[...]
    block = dots(
        scaled * res1, res1 * (part_w[...] - alpha0 * second[...]), scaled * image0
    )
    summing = start_sum(1, 0, block)
    for copy in exchange:
        copy.wait_recv()
    add_received(2, second)
    summing = start_sum(1, 1, end_sum(1, 0, summing))
    summing = start_sum(1, 2, end_sum(1, 1, summing))
    totals = jnp.sum(end_sum(1, 2, summing), axis=1, keepdims=True)
    norm1 = totals[0:1]
    beta = norm1 / norm0
    energy1 = totals[1:2] + beta * (2.0 * totals[2:3] + beta * energy0)
    alpha1 = norm1 / energy1

    res0 = resid[...]
    image0 = image[...]
    res1 = res0 - alpha0 * image0
    image1 = (image0 - alpha0 * second[...]) + beta * image0
    solved = alpha0 * res0 + alpha1 * (res1 + beta * res0)
    left = res1 - alpha1 * image1
    sol_ref[...] = solved[0:ROWS]
    res_ref[...] = left[0:ROWS]
    for copy in copies:
        copy.wait_send()


def solution(mesh):
    n_px = mesh.shape["px"]
    n_py = mesh.shape["py"]
    low_py = 4 if n_py >= 16 else 2
    count = 3 * 8 + 2 * ((2 * low_py - 1) + (n_px // 2 - 1) + (n_py // low_py - 1))
    coef, ahead, back = tables()

    def body(right_side, geometry, shift, node_order, elem_counts, share_lists):
        vmem = pl.BlockSpec(memory_space=pltpu.VMEM)
        plane = jax.ShapeDtypeStruct((ROWS, LANES), jnp.float32)
        vector = pltpu.VMEM((PAD, LANES), jnp.float32)
        solved, left = pl.pallas_call(
            functools.partial(kernel, n_px, n_py),
            out_shape=(plane, plane),
            in_specs=[vmem] * 9,
            out_specs=(vmem, vmem),
            scratch_shapes=[
                vector,
                vector,
                vector,
                vector,
                pltpu.VMEM((8 * ELEMS + 8, LANES), jnp.float32),
                pltpu.VMEM((8 * ELEMS + 8, LANES), jnp.float32),
                pltpu.VMEM((3, PAD, LANES), jnp.float32),
                pltpu.VMEM((8 * ELEMS + 8, LANES), jnp.int32),
                pltpu.VMEM((80, LANES), jnp.int32),
                pltpu.VMEM((8, LANES), jnp.int32),
                pltpu.VMEM((8, LANES), jnp.int32),
                vector,
                pltpu.VMEM((8, LANES), jnp.float32),
                pltpu.VMEM((3 * TURN, LANES), jnp.float32),
                pltpu.VMEM((3 * TURN, LANES), jnp.float32),
                pltpu.VMEM((3 * 32, LANES), jnp.float32),
                pltpu.VMEM((2, 3, 8, 8, LANES), jnp.float32),
                pltpu.SemaphoreType.DMA((count,)),
                pltpu.SemaphoreType.DMA((count,)),
            ],
            compiler_params=pltpu.CompilerParams(
                collective_id=0, has_side_effects=True, vmem_limit_bytes=32 * 2**20
            ),
            cost_estimate=pl.CostEstimate(
                flops=10**8, bytes_accessed=2 * 10**6, transcendentals=0
            ),
        )(
            right_side.reshape(ROWS, LANES),
            geometry[0, 0],
            shift.reshape(ELEMS, 1),
            node_order[0, 0],
            elem_counts,
            share_lists[0, 0],
            jnp.asarray(coef),
            jnp.asarray(ahead),
            jnp.asarray(back),
        )
        shape = (1, 1, ROWS * LANES)
        return solved.reshape(shape), left.reshape(shape)

    return jax.shard_map(
        body,
        mesh=mesh,
        in_specs=(
            P("px", "py", None),
            P("px", "py", None, None, None),
            P("px", "py", None),
            P("px", "py", None, None),
            P("px", "py"),
            P("px", "py", None, None),
        ),
        out_specs=(P("px", "py", None), P("px", "py", None)),
        check_vma=False,
    )
```

```python
import functools

import jax
import jax.numpy as jnp
import numpy as np
from jax import lax
from jax.experimental import pallas as pl
from jax.experimental.pallas import tpu as pltpu
from jax.sharding import PartitionSpec as P

STRIDE = 344
FACE = 1280
DIAG = 128
ELEMS = 48
LANES = 128
ROWS = 129
PAD = 136
FACE_ROWS = FACE // LANES
TURN = 80
ROW_OF = [e * STRIDE // LANES for e in range(ELEMS)]
LOWER = (1, 3, 2, 3)
UPPER = (0, 2, 0, 1)
FACE_STEPS = ((1, 0), (-1, 0), (0, 1), (0, -1))
DIAG_STEPS = ((1, 1), (1, -1), (-1, 1), (-1, -1))
DIAG_LIST = (0, 0, 1, 1)


def gll_derivative():
    degree = 7
    points = np.array(
        [
            -1.0,
            -0.8717401485096066,
            -0.5917001814331423,
            -0.2092992179024789,
            0.2092992179024789,
            0.5917001814331423,
            0.8717401485096066,
            1.0,
        ]
    )
    before = np.ones(8)
    current = points * 1.0
    for order in range(1, degree):
        following = ((2 * order + 1) * points * current - order * before) / (order + 1)
        before = current
        current = following
    same = np.arange(8)[:, None] == np.arange(8)[None, :]
    spacing = np.where(same, 1.0, points[:, None] - points[None, :])
    matrix = np.where(same, 0.0, current[:, None] / (current[None, :] * spacing))
    corner = np.array([-14.0, 0.0, 0.0, 0.0, 0.0, 0.0, 0.0, 14.0])
    return matrix + np.where(same, corner[:, None], 0.0)


def tables():
    deriv = gll_derivative()
    half = np.arange(LANES) // 64

    def lanes_of(matrix):
        rows = []
        for out in range(4):
            for src in range(4):
                rows.append(matrix[2 * out + half, 2 * src + half])
                rows.append(matrix[2 * out + half, 2 * src + 1 - half])
        return np.stack(rows)

    coef = np.concatenate([lanes_of(deriv), lanes_of(deriv.T)])
    second = np.kron(np.eye(2), np.kron(deriv, np.eye(8)))
    third = np.kron(np.eye(16), deriv)
    ahead = np.concatenate([second.T, third.T], axis=1)
    back = np.concatenate([second, third], axis=0)
    return tuple(np.asarray(t, np.float32) for t in (coef, ahead, back))


def take_lanes(values, lanes):
    return jnp.take_along_axis(values, lanes, axis=1, mode="promise_in_bounds")


def pick(sources, index):
    high = index >> 7
    lanes = index & 127
    total = None
    for j, source in enumerate(sources):
        term = jnp.where(high == j, take_lanes(source, lanes), 0.0)
        total = term if total is None else total + term
    return total


def eight(row):
    return jnp.broadcast_to(row, (8, row.shape[1]))


def iota(shape, dim):
    return lax.broadcasted_iota(jnp.int32, shape, dim)


def one_hot_lanes(low):
    return jnp.where(low == iota((LANES, low.shape[1]), 0), 1.0, 0.0).astype(jnp.bfloat16)


def over_lanes(left, right):
    return lax.dot_general(
        left, right, (((1,), (1,)), ((), ())), preferred_element_type=jnp.float32
    )


def inverse_rows(high, low, groups):
    count = high.shape[1]
    number = iota((groups, count), 1) + 1
    hit = high == iota((groups, count), 0)
    tens = jnp.where(hit, number >> 4, 0).astype(jnp.float32)
    ones = jnp.where(hit, number & 15, 0).astype(jnp.float32)
    left = jnp.concatenate([tens, ones], axis=0).astype(jnp.bfloat16)
    found = over_lanes(left, one_hot_lanes(low))
    return (16.0 * found[:groups] + found[groups:]).astype(jnp.int32) - 1


def kernel(
    n_px,
    n_py,
    rhs_hbm,
    geo_hbm,
    shift_hbm,
    order_hbm,
    count_ref,
    lists_hbm,
    coef_hbm,
    ahead_hbm,
    back_hbm,
    sol_ref,
    res_ref,
    rhs_ref,
    geo_ref,
    shift_ref,
    order_ref,
    lists_ref,
    coef_ref,
    ahead_ref,
    back_ref,
    factors,
    resid,
    image,
    second,
    part_w,
    windows,
    spread,
    sums,
    elem_inv,
    face_inv,
    cross_inv,
    wrap_inv,
    inv_mult,
    cross_src,
    send,
    recv,
    recv_diag,
    red,
    send_sem,
    recv_sem,
    load_sem,
):
    loads = {}
    for number, (name, src, dst) in enumerate(
        (
            ("lists", lists_hbm, lists_ref),
            ("rhs", rhs_hbm, rhs_ref),
            ("order", order_hbm, order_ref),
            ("shift", shift_hbm, shift_ref),
            ("ahead", ahead_hbm, ahead_ref),
            ("geo", geo_hbm, geo_ref),
            ("back", back_hbm, back_ref),
            ("coef", coef_hbm, coef_ref),
        )
    ):
        loads[name] = pltpu.make_async_copy(src, dst, load_sem.at[number])
        loads[name].start()

    px = lax.axis_index("px")
    py = lax.axis_index("py")

    def moved(step_x, step_y):
        return (lax.rem(px + step_x + n_px, n_px), lax.rem(py + step_y + n_py, n_py))

    sizes = (n_px, n_py)

    def place(stage):
        return px if stage == 0 else py

    def partners(stage):
        if stage == 0:
            return [(lax.rem(px + d, n_px), py) for d in range(1, n_px)]
        return [(px, lax.rem(py + d, n_py)) for d in range(1, n_py)]

    everyone = [moved(*step) for step in FACE_STEPS + DIAG_STEPS]
    everyone += partners(0) + partners(1)
    barrier = pltpu.get_barrier_semaphore()
    for other in everyone:
        pl.semaphore_signal(
            barrier, inc=1, device_id=other, device_id_type=pl.DeviceIdType.MESH
        )

    copies = []

    def start_copy(src, dst, other):
        number = len(copies)
        copy = pltpu.make_async_remote_copy(
            src_ref=src,
            dst_ref=dst,
            send_sem=send_sem.at[number],
            recv_sem=recv_sem.at[number],
            device_id=other,
            device_id_type=pl.DeviceIdType.MESH,
        )
        copy.start()
        copies.append(copy)
        return copy

    def start_exchange(turn):
        started = []
        for f, step in enumerate(FACE_STEPS):
            started.append(
                start_copy(
                    send.at[pl.ds(TURN * turn + 16 * f, 16)],
                    recv.at[pl.ds(TURN * turn + 16 * (f ^ 1), 16)],
                    moved(*step),
                )
            )
        for d, step in enumerate(DIAG_STEPS):
            started.append(
                start_copy(
                    send.at[pl.ds(TURN * turn + 16 * DIAG_LIST[d] + 8, 8)],
                    recv_diag.at[pl.ds(32 * turn + 8 * (3 - d), 8)],
                    moved(*step),
                )
            )
        return started

    def start_sum(turn, stage, row):
        first = turn * (n_px + n_py) + stage * n_px
        mine = first + place(stage)
        red[pl.ds(mine, 1)] = row[None]
        return [start_copy(red.at[mine], red.at[mine], other) for other in partners(stage)]

    def end_sum(turn, stage, started):
        first = turn * (n_px + n_py) + stage * n_px
        for copy in started:
            copy.wait_recv()
        sums_of = [red[first + slot] for slot in range(sizes[stage])]
        while len(sums_of) > 1:
            sums_of = [x + y for x, y in zip(sums_of[::2], sums_of[1::2])]
        return sums_of[0]

    live = count_ref[...]

    def fill_send(turn, source):
        for i in range(FACE_ROWS):
            index = lists_ref[:, i * LANES : (i + 1) * LANES]
            found = pick(
                [source[pl.ds(j, 4, stride=FACE_ROWS), :] for j in range(FACE_ROWS)], index
            )
            send[pl.ds(TURN * turn + i, 4, stride=16), :] = found
        first = 4 * FACE_ROWS
        for part, regions in enumerate((LOWER, UPPER)):
            for f, q in enumerate(regions):
                cross_src[4 * part + f : 4 * part + f + 1, :] = source[first + q : first + q + 1, :]
        for part in range(2):
            at = FACE + part * DIAG
            found = pick(
                [cross_src[4 * part : 4 * part + 4, :]], lists_ref[:, at : at + DIAG]
            )
            send[pl.ds(TURN * turn + FACE_ROWS + part, 4, stride=16), :] = found

    def add_received(turn, target):
        def sent_row(i):
            return recv[pl.ds(TURN * turn + i, 4, stride=16), :]

        def diagonal_row(q, i):
            at = 32 * turn + 8 * q + i
            return recv_diag[at : at + 1, :]

        for i in range(FACE_ROWS):
            index = face_inv[pl.ds(i, 4, stride=16), :]
            found = pick([sent_row(j) for j in range(FACE_ROWS)], index)
            target[pl.ds(i, 4, stride=FACE_ROWS), :] += found
        blank = jnp.zeros((2, LANES), jnp.float32)
        lower = sent_row(FACE_ROWS) + jnp.concatenate(
            [blank, diagonal_row(2, 2), diagonal_row(3, 3)], axis=0
        )
        upper = sent_row(FACE_ROWS + 1) + jnp.concatenate(
            [blank, diagonal_row(0, 2), diagonal_row(1, 3)], axis=0
        )
        lower = pick([lower], cross_inv[0:4, :])
        upper = pick([upper], cross_inv[4:8, :])
        first = 4 * FACE_ROWS
        for part, regions in ((lower, LOWER), (upper, UPPER)):
            for f, q in enumerate(regions):
                target[first + q : first + q + 1, :] += part[f : f + 1]

    element = iota((ELEMS, LANES), 0)
    offset = (element * STRIDE) & 127
    is_last = element == live - 1

    def orders(c):
        return order_ref[:, c * LANES : (c + 1) * LANES]

    def last_row(values):
        return jnp.sum(jnp.where(is_last, values, jnp.zeros_like(values)), axis=0, keepdims=True)

    def set_up():
        for f in range(4):
            row = lists_ref[f : f + 1, 0:FACE]
            face_inv[16 * f : 16 * f + 16, :] = inverse_rows(row >> 7, row & 127, 16)
            for part in range(2):
                at = FACE + part * DIAG
                row = lists_ref[f : f + 1, at : at + DIAG]
                number = (iota((8, DIAG), 1) + 1).astype(jnp.float32).astype(jnp.bfloat16)
                found = over_lanes(number, one_hot_lanes(row))
                cross_inv[4 * part + f : 4 * part + f + 1, :] = found[0:1].astype(jnp.int32) - 1
        inv_mult[...] = jnp.ones_like(inv_mult)
        for f in range(4):
            named = face_inv[16 * f : 16 * f + FACE_ROWS, :] >= 0
            inv_mult[f * FACE_ROWS : (f + 1) * FACE_ROWS, :] = jnp.where(named, 0.5, 1.0)
        for q in range(4):
            copies_of = jnp.ones((1, LANES), jnp.float32)
            for part, regions in enumerate((LOWER, UPPER)):
                for f, region in enumerate(regions):
                    if region == q:
                        row = cross_inv[4 * part + f : 4 * part + f + 1, :]
                        copies_of = copies_of + jnp.where(row >= 0, 1.5, 0.0)
            at = 4 * FACE_ROWS + q
            inv_mult[at : at + 1, :] = 1.0 / copies_of

        @pl.loop(0, ELEMS // 8)
        def _(group):
            block = order_ref[pl.ds(pl.multiple_of(8 * group, 8), 8), :]
            for s in range(8):
                e = 8 * group + s
                row = block[s : s + 1]
                shifted = row + lax.rem(e * STRIDE, LANES)
                own = jnp.where(live <= e, 0, jnp.where(live == e + 1, STRIDE, 4 * LANES))
                high = jnp.where(row >= own, 7, shifted >> 7)
                elem_inv[pl.ds(pl.multiple_of(8 * e, 8), 8), :] = inverse_rows(
                    high, shifted & 127, 8
                )

        wrapped = jnp.concatenate([last_row(orders(c)) for c in range(4)], axis=1) - STRIDE
        wrap_inv[...] = inverse_rows(wrapped >> 7, wrapped & 127, 8)

    def derivative(chunks, first):
        swapped = [pltpu.roll(u, 64, 1) for u in chunks]
        result = []
        for out in range(4):
            total = None
            for src in range(4):
                at = first + (out * 4 + src) * 2
                term = coef_ref[at : at + 1, :] * chunks[src]
                total = term if total is None else total + term
                total = total + coef_ref[at + 1 : at + 2, :] * swapped[src]
            result.append(total)
        return result

    def stacked(k):
        return jnp.concatenate(
            [geo_ref[k, :, c * LANES : (c + 1) * LANES] for c in range(4)], axis=0
        )

    def operate(source):
        for e, row in enumerate(ROW_OF):
            windows[8 * e : 8 * e + 8, :] = source[row : row + 8, :]
        rows = [windows[pl.ds(k, ELEMS, stride=8), :] for k in range(5)]
        chunks = []
        for c in range(4):
            order = orders(c)
            around = pick(
                [eight(source[0:1, :]), eight(source[1:2, :])], eight(last_row(order)) - STRIDE
            )[0:1]
            values = pick(rows, order + offset)
            chunks.append(jnp.where(is_last & (order >= STRIDE), around, values))
        exact = lax.Precision.HIGHEST
        narrow = jnp.concatenate(chunks, axis=0)
        grads = jnp.dot(
            narrow, ahead_ref[...], precision=exact, preferred_element_type=jnp.float32
        )
        fluxes = jnp.concatenate(
            [stacked(1) * grads[:, :LANES], stacked(2) * grads[:, LANES:]], axis=1
        )
        terms = jnp.dot(
            fluxes, back_ref[...], precision=exact, preferred_element_type=jnp.float32
        )
        grad = derivative(chunks, 0)
        grad = [geo_ref[0, :, c * LANES : (c + 1) * LANES] * grad[c] for c in range(4)]
        first = derivative(grad, 32)
        factor = factors[...]
        result = [
            terms[c * ELEMS : (c + 1) * ELEMS] + first[c] + factor * chunks[c] for c in range(4)
        ]
        for k in range(5):
            spread[pl.ds(k, ELEMS, stride=8), :] = pick(
                result, elem_inv[pl.ds(k, ELEMS, stride=8), :]
            )
        for e, row in enumerate(ROW_OF):
            sums[e % 3, row : row + 8, :] = spread[8 * e : 8 * e + 8, :]
        sums[0, 0:8, :] += pick([eight(last_row(r)) for r in result], wrap_inv[...])
        return sums[0] + sums[1] + sums[2]

    def dots(*products):
        lane = iota((1, LANES), 1)
        row = jnp.zeros((1, LANES), jnp.float32)
        for k, product in enumerate(products):
            total = jnp.sum(jnp.sum(product, axis=0, keepdims=True), axis=1, keepdims=True)
            row = jnp.where(lane == k, total, row)
        return row

    send[...] = jnp.zeros_like(send)
    spread[...] = jnp.zeros_like(spread)
    sums[...] = jnp.zeros_like(sums)
    resid[...] = jnp.zeros_like(resid)
    loads["lists"].wait()
    loads["rhs"].wait()
    for i in range(ROWS):
        resid[i : i + 1, :] = rhs_ref[:, i * LANES : (i + 1) * LANES]
    slot = iota((ROWS, LANES), 0) * LANES + iota((ROWS, LANES), 1)
    resid[0:ROWS, :] = jnp.where(slot < live * STRIDE, resid[0:ROWS, :], 0.0)
    fill_send(0, resid)
    pl.semaphore_wait(barrier, len(everyone))
    exchange = start_exchange(0)
    loads["order"].wait()
    loads["shift"].wait()
    set_up()
    same = iota((ELEMS, ELEMS), 0) == iota((ELEMS, ELEMS), 1)
    column = jnp.sum(jnp.where(same, shift_ref[...], 0.0), axis=1, keepdims=True)
    factors[...] = jnp.broadcast_to(column, (ELEMS, LANES))
    for name in ("ahead", "geo", "back", "coef"):
        loads[name].wait()
    for copy in exchange:
        copy.wait_recv()
    add_received(0, resid)

    part_w[...] = operate(resid)
    res0 = resid[...]
    summing = start_sum(0, 0, dots(res0 * res0 * inv_mult[...], res0 * part_w[...]))
    image[...] = part_w[...]
    fill_send(1, image)
    exchange = start_exchange(1)
    summing = start_sum(0, 1, end_sum(0, 0, summing))
    for copy in exchange:
        copy.wait_recv()
    add_received(1, image)

    second[...] = operate(image)
    fill_send(2, second)
    exchange = start_exchange(2)
    totals = end_sum(0, 1, summing)
    norm0 = totals[:, 0:1]
    energy0 = totals[:, 1:2]
    alpha0 = norm0 / energy0

    res0 = resid[...]
    image0 = image[...]
    res1 = res0 - alpha0 * image0
    scaled = res1 * inv_mult[...]
    row = dots(scaled * res1, res1 * (part_w[...] - alpha0 * second[...]), scaled * image0)
    summing = start_sum(1, 0, row)
    for copy in exchange:
        copy.wait_recv()
    add_received(2, second)
    earlier = list(copies)
    summing = start_sum(1, 1, end_sum(1, 0, summing))
    for copy in earlier:
        copy.wait_send()
    totals = end_sum(1, 1, summing)
    norm1 = totals[:, 0:1]
    beta = norm1 / norm0
    energy1 = totals[:, 1:2] + beta * (2.0 * totals[:, 2:3] + beta * energy0)
    alpha1 = norm1 / energy1

    res0 = resid[...]
    image0 = image[...]
    res1 = res0 - alpha0 * image0
    image1 = (image0 - alpha0 * second[...]) + beta * image0
    solved = alpha0 * res0 + alpha1 * (res1 + beta * res0)
    left = res1 - alpha1 * image1
    sol_ref[...] = solved[0:ROWS]
    res_ref[...] = left[0:ROWS]
    for copy in summing:
        copy.wait_send()


def solution(mesh):
    n_px = mesh.shape["px"]
    n_py = mesh.shape["py"]
    count = 3 * 8 + 2 * (n_px - 1 + n_py - 1)
    coef, ahead, back = tables()

    def body(right_side, geometry, shift, node_order, elem_counts, share_lists):
        vmem = pl.BlockSpec(memory_space=pltpu.VMEM)
        hbm = pl.BlockSpec(memory_space=pltpu.HBM)
        plane = jax.ShapeDtypeStruct((ROWS, LANES), jnp.float32)
        vector = pltpu.VMEM((PAD, LANES), jnp.float32)
        solved, left = pl.pallas_call(
            functools.partial(kernel, n_px, n_py),
            out_shape=(plane, plane),
            in_specs=[hbm] * 4 + [vmem] + [hbm] * 4,
            out_specs=(vmem, vmem),
            scratch_shapes=[
                pltpu.VMEM((1, ROWS * LANES), jnp.float32),
                pltpu.VMEM((3, ELEMS, 4 * LANES), jnp.float32),
                pltpu.VMEM((1, ELEMS), jnp.float32),
                pltpu.VMEM((ELEMS, 4 * LANES), jnp.int32),
                pltpu.VMEM((4, FACE + 2 * DIAG), jnp.int32),
                pltpu.VMEM(coef.shape, jnp.float32),
                pltpu.VMEM(ahead.shape, jnp.float32),
                pltpu.VMEM(back.shape, jnp.float32),
                pltpu.VMEM((ELEMS, LANES), jnp.float32),
                vector,
                vector,
                vector,
                vector,
                pltpu.VMEM((8 * ELEMS + 8, LANES), jnp.float32),
                pltpu.VMEM((8 * ELEMS + 8, LANES), jnp.float32),
                pltpu.VMEM((3, PAD, LANES), jnp.float32),
                pltpu.VMEM((8 * ELEMS + 8, LANES), jnp.int32),
                pltpu.VMEM((80, LANES), jnp.int32),
                pltpu.VMEM((8, LANES), jnp.int32),
                pltpu.VMEM((8, LANES), jnp.int32),
                vector,
                pltpu.VMEM((8, LANES), jnp.float32),
                pltpu.VMEM((3 * TURN, LANES), jnp.float32),
                pltpu.VMEM((3 * TURN, LANES), jnp.float32),
                pltpu.VMEM((3 * 32, LANES), jnp.float32),
                pltpu.VMEM((2 * (n_px + n_py), 1, LANES), jnp.float32),
                pltpu.SemaphoreType.DMA((count,)),
                pltpu.SemaphoreType.DMA((count,)),
                pltpu.SemaphoreType.DMA((8,)),
            ],
            compiler_params=pltpu.CompilerParams(
                collective_id=0, has_side_effects=True, vmem_limit_bytes=60 * 2**20
            ),
            cost_estimate=pl.CostEstimate(
                flops=10**8, bytes_accessed=2 * 10**6, transcendentals=0
            ),
        )(
            right_side[0],
            geometry[0, 0],
            shift[0],
            node_order[0, 0],
            elem_counts,
            share_lists[0, 0],
            jnp.asarray(coef),
            jnp.asarray(ahead),
            jnp.asarray(back),
        )
        shape = (1, 1, ROWS * LANES)
        return solved.reshape(shape), left.reshape(shape)

    return jax.shard_map(
        body,
        mesh=mesh,
        in_specs=(
            P("px", "py", None),
            P("px", "py", None, None, None),
            P("px", "py", None),
            P("px", "py", None, None),
            P("px", "py"),
            P("px", "py", None, None),
        ),
        out_specs=(P("px", "py", None), P("px", "py", None)),
        check_vma=False,
    )
```

```python
import functools

import jax
import jax.numpy as jnp
import numpy as np
from jax import lax
from jax.experimental import pallas as pl
from jax.experimental.pallas import tpu as pltpu
from jax.sharding import PartitionSpec as P

STRIDE = 344
FACE = 1280
DIAG = 128
ELEMS = 48
LANES = 128
ROWS = 129
PAD = 136
FACE_ROWS = FACE // LANES
TURN = 80
ROW_OF = [e * STRIDE // LANES for e in range(ELEMS)]
LOWER = (1, 3, 2, 3)
UPPER = (0, 2, 0, 1)
FACE_STEPS = ((1, 0), (-1, 0), (0, 1), (0, -1))
DIAG_STEPS = ((1, 1), (1, -1), (-1, 1), (-1, -1))
DIAG_LIST = (0, 0, 1, 1)


def gll_derivative():
    degree = 7
    points = np.array(
        [
            -1.0,
            -0.8717401485096066,
            -0.5917001814331423,
            -0.2092992179024789,
            0.2092992179024789,
            0.5917001814331423,
            0.8717401485096066,
            1.0,
        ]
    )
    before = np.ones(8)
    current = points * 1.0
    for order in range(1, degree):
        following = ((2 * order + 1) * points * current - order * before) / (order + 1)
        before = current
        current = following
    same = np.arange(8)[:, None] == np.arange(8)[None, :]
    spacing = np.where(same, 1.0, points[:, None] - points[None, :])
    matrix = np.where(same, 0.0, current[:, None] / (current[None, :] * spacing))
    corner = np.array([-14.0, 0.0, 0.0, 0.0, 0.0, 0.0, 0.0, 14.0])
    return matrix + np.where(same, corner[:, None], 0.0)


def tables():
    deriv = gll_derivative()
    half = np.arange(LANES) // 64

    def lanes_of(matrix):
        rows = []
        for out in range(4):
            for src in range(4):
                rows.append(matrix[2 * out + half, 2 * src + half])
                rows.append(matrix[2 * out + half, 2 * src + 1 - half])
        return np.stack(rows)

    coef = np.concatenate([lanes_of(deriv), lanes_of(deriv.T)])
    second = np.kron(np.eye(2), np.kron(deriv, np.eye(8)))
    third = np.kron(np.eye(16), deriv)
    ahead = np.concatenate([second.T, third.T], axis=1)
    back = np.concatenate([second, third], axis=0)
    return tuple(np.asarray(t, np.float32) for t in (coef, ahead, back))


def take_lanes(values, lanes):
    return jnp.take_along_axis(values, lanes, axis=1, mode="promise_in_bounds")


def pick(sources, index):
    high = index >> 7
    lanes = index & 127
    total = None
    for j, source in enumerate(sources):
        found = take_lanes(source, lanes)
        total = jnp.where(high == j, found, 0.0 if total is None else total)
    return total


def eight(row):
    return jnp.broadcast_to(row, (8, row.shape[1]))


def iota(shape, dim):
    return lax.broadcasted_iota(jnp.int32, shape, dim)


def one_hot_lanes(low):
    return jnp.where(low == iota((LANES, low.shape[1]), 0), 1.0, 0.0).astype(jnp.bfloat16)


def over_lanes(left, right):
    return lax.dot_general(
        left, right, (((1,), (1,)), ((), ())), preferred_element_type=jnp.float32
    )


def inverse_rows(high, low, groups):
    count = high.shape[1]
    number = iota((groups, count), 1) + 1
    hit = high == iota((groups, count), 0)
    tens = jnp.where(hit, number >> 4, 0).astype(jnp.float32)
    ones = jnp.where(hit, number & 15, 0).astype(jnp.float32)
    left = jnp.concatenate([tens, ones], axis=0).astype(jnp.bfloat16)
    found = over_lanes(left, one_hot_lanes(low))
    return (16.0 * found[:groups] + found[groups:]).astype(jnp.int32) - 1


def kernel(
    n_px,
    n_py,
    rhs_hbm,
    geo_hbm,
    shift_hbm,
    order_hbm,
    count_ref,
    lists_hbm,
    coef_hbm,
    ahead_hbm,
    back_hbm,
    sol_ref,
    res_ref,
    rhs_ref,
    geo_ref,
    shift_ref,
    order_ref,
    lists_ref,
    coef_ref,
    ahead_ref,
    back_ref,
    factors,
    resid,
    image,
    second,
    part_w,
    windows,
    spread,
    sums,
    elem_inv,
    face_inv,
    cross_inv,
    wrap_inv,
    inv_mult,
    cross_src,
    stack,
    list_idx,
    inv_idx,
    wrap_idx,
    send,
    recv,
    recv_diag,
    red,
    send_sem,
    recv_sem,
    load_sem,
):
    loads = {}
    for number, (name, src, dst) in enumerate(
        (
            ("lists", lists_hbm, lists_ref),
            ("rhs", rhs_hbm, rhs_ref),
            ("order", order_hbm, order_ref),
            ("shift", shift_hbm, shift_ref),
            ("ahead", ahead_hbm, ahead_ref),
            ("geo", geo_hbm, geo_ref),
            ("back", back_hbm, back_ref),
            ("coef", coef_hbm, coef_ref),
        )
    ):
        loads[name] = pltpu.make_async_copy(src, dst, load_sem.at[number])
        loads[name].start()

    px = lax.axis_index("px")
    py = lax.axis_index("py")

    def moved(step_x, step_y):
        return (lax.rem(px + step_x + n_px, n_px), lax.rem(py + step_y + n_py, n_py))

    sizes = (n_px, n_py)

    def place(stage):
        return px if stage == 0 else py

    def partners(stage):
        if stage == 0:
            return [(lax.rem(px + d, n_px), py) for d in range(1, n_px)]
        return [(px, lax.rem(py + d, n_py)) for d in range(1, n_py)]

    everyone = [moved(*step) for step in FACE_STEPS + DIAG_STEPS]
    everyone += partners(0) + partners(1)
    barrier = pltpu.get_barrier_semaphore()
    for other in everyone:
        pl.semaphore_signal(
            barrier, inc=1, device_id=other, device_id_type=pl.DeviceIdType.MESH
        )

    copies = []

    def start_copy(src, dst, other):
        number = len(copies)
        copy = pltpu.make_async_remote_copy(
            src_ref=src,
            dst_ref=dst,
            send_sem=send_sem.at[number],
            recv_sem=recv_sem.at[number],
            device_id=other,
            device_id_type=pl.DeviceIdType.MESH,
        )
        copy.start()
        copies.append(copy)
        return copy

    def start_exchange(turn):
        started = []
        for f, step in enumerate(FACE_STEPS):
            started.append(
                start_copy(
                    send.at[pl.ds(TURN * turn + 16 * f, 16)],
                    recv.at[pl.ds(TURN * turn + 16 * (f ^ 1), 16)],
                    moved(*step),
                )
            )
        for d, step in enumerate(DIAG_STEPS):
            started.append(
                start_copy(
                    send.at[pl.ds(TURN * turn + 16 * DIAG_LIST[d] + 8, 8)],
                    recv_diag.at[pl.ds(32 * turn + 8 * (3 - d), 8)],
                    moved(*step),
                )
            )
        return started

    def start_sum(turn, stage, row):
        first = turn * (n_px + n_py) + stage * n_px
        mine = first + place(stage)
        red[pl.ds(mine, 1)] = row[None]
        return [start_copy(red.at[mine], red.at[mine], other) for other in partners(stage)]

    def end_sum(turn, stage, started):
        first = turn * (n_px + n_py) + stage * n_px
        for copy in started:
            copy.wait_recv()
        sums_of = [red[first + slot] for slot in range(sizes[stage])]
        while len(sums_of) > 1:
            sums_of = [x + y for x, y in zip(sums_of[::2], sums_of[1::2])]
        return sums_of[0]

    live = count_ref[...]

    half = FACE_ROWS // 2

    def pair_up(target, at, upper, lower):
        target[at : at + 4, :] = upper
        target[at + 4 : at + 8, :] = lower

    def stack_rows(source, first, step):
        for j in range(FACE_ROWS):
            rows = source[pl.ds(first + j, 4, stride=step), :]
            pair_up(stack, 8 * j, rows, rows)
        return [stack[8 * j : 8 * j + 8, :] for j in range(FACE_ROWS)]

    def fill_send(turn, source):
        rows = stack_rows(source, 0, FACE_ROWS)
        for i in range(half):
            found = pick(rows, list_idx[8 * i : 8 * i + 8, :])
            send[pl.ds(TURN * turn + i, 4, stride=16), :] = found[0:4]
            send[pl.ds(TURN * turn + i + half, 4, stride=16), :] = found[4:8]
        first = 4 * FACE_ROWS
        for at, q in enumerate(LOWER + UPPER):
            cross_src[at : at + 1, :] = source[first + q : first + q + 1, :]
        found = pick([cross_src[...]], list_idx[8 * half : 8 * half + 8, :])
        send[pl.ds(TURN * turn + FACE_ROWS, 4, stride=16), :] = found[0:4]
        send[pl.ds(TURN * turn + FACE_ROWS + 1, 4, stride=16), :] = found[4:8]

    def add_received(turn, target):
        rows = stack_rows(recv, TURN * turn, 16)
        for i in range(half):
            found = pick(rows, inv_idx[8 * i : 8 * i + 8, :])
            target[pl.ds(i, 4, stride=FACE_ROWS), :] += found[0:4]
            target[pl.ds(i + half, 4, stride=FACE_ROWS), :] += found[4:8]
        for part in range(2):
            at = TURN * turn + FACE_ROWS + part
            cross_src[4 * part : 4 * part + 4, :] = recv[pl.ds(at, 4, stride=16), :]
        for row, q, i in ((2, 2, 2), (3, 3, 3), (6, 0, 2), (7, 1, 3)):
            at = 32 * turn + 8 * q + i
            cross_src[row : row + 1, :] += recv_diag[at : at + 1, :]
        found = pick([cross_src[...]], cross_inv[...])
        first = 4 * FACE_ROWS
        for at, q in enumerate(LOWER + UPPER):
            target[first + q : first + q + 1, :] += found[at : at + 1]

    element = iota((ELEMS, LANES), 0)
    offset = (element * STRIDE) & 127
    is_last = element == live - 1

    def orders(c):
        return order_ref[:, c * LANES : (c + 1) * LANES]

    def last_row(values):
        return jnp.sum(jnp.where(is_last, values, jnp.zeros_like(values)), axis=0, keepdims=True)

    def set_up():
        for f in range(4):
            row = lists_ref[f : f + 1, 0:FACE]
            face_inv[16 * f : 16 * f + 16, :] = inverse_rows(row >> 7, row & 127, 16)
            for part in range(2):
                at = FACE + part * DIAG
                row = lists_ref[f : f + 1, at : at + DIAG]
                number = (iota((8, DIAG), 1) + 1).astype(jnp.float32).astype(jnp.bfloat16)
                found = over_lanes(number, one_hot_lanes(row))
                cross_inv[4 * part + f : 4 * part + f + 1, :] = found[0:1].astype(jnp.int32) - 1
        for i in range(half):
            pair_up(
                inv_idx,
                8 * i,
                face_inv[pl.ds(i, 4, stride=16), :],
                face_inv[pl.ds(i + half, 4, stride=16), :],
            )
        inv_mult[...] = jnp.ones_like(inv_mult)
        for f in range(4):
            named = face_inv[16 * f : 16 * f + FACE_ROWS, :] >= 0
            inv_mult[f * FACE_ROWS : (f + 1) * FACE_ROWS, :] = jnp.where(named, 0.5, 1.0)
        for q in range(4):
            copies_of = jnp.ones((1, LANES), jnp.float32)
            for part, regions in enumerate((LOWER, UPPER)):
                for f, region in enumerate(regions):
                    if region == q:
                        row = cross_inv[4 * part + f : 4 * part + f + 1, :]
                        copies_of = copies_of + jnp.where(row >= 0, 1.5, 0.0)
            at = 4 * FACE_ROWS + q
            inv_mult[at : at + 1, :] = 1.0 / copies_of

        @pl.loop(0, ELEMS // 8)
        def _(group):
            block = order_ref[pl.ds(pl.multiple_of(8 * group, 8), 8), :]
            for s in range(8):
                e = 8 * group + s
                row = block[s : s + 1]
                shifted = row + lax.rem(e * STRIDE, LANES)
                own = jnp.where(live <= e, 0, jnp.where(live == e + 1, STRIDE, 4 * LANES))
                high = jnp.where(row >= own, 7, shifted >> 7)
                elem_inv[pl.ds(pl.multiple_of(8 * e, 8), 8), :] = inverse_rows(
                    high, shifted & 127, 8
                )

        wrapped = jnp.concatenate([last_row(orders(c)) for c in range(4)], axis=1) - STRIDE
        wrap_inv[...] = inverse_rows(wrapped >> 7, wrapped & 127, 8)
        wrap_idx[...] = eight(wrapped)

    def derivative(chunks, first):
        swapped = [pltpu.roll(u, 64, 1) for u in chunks]
        result = []
        for out in range(4):
            total = None
            for src in range(4):
                at = first + (out * 4 + src) * 2
                term = coef_ref[at : at + 1, :] * chunks[src]
                total = term if total is None else total + term
                total = total + coef_ref[at + 1 : at + 2, :] * swapped[src]
            result.append(total)
        return result

    def stacked(k):
        return jnp.concatenate(
            [geo_ref[k, :, c * LANES : (c + 1) * LANES] for c in range(4)], axis=0
        )

    def operate(source):
        for e, row in enumerate(ROW_OF):
            windows[8 * e : 8 * e + 8, :] = source[row : row + 8, :]
        rows = [windows[pl.ds(k, ELEMS, stride=8), :] for k in range(5)]
        chunks = []
        for c in range(4):
            order = orders(c)
            around = pick(
                [eight(source[0:1, :]), eight(source[1:2, :])],
                wrap_idx[:, c * LANES : (c + 1) * LANES],
            )[0:1]
            values = pick(rows, order + offset)
            chunks.append(jnp.where(is_last & (order >= STRIDE), around, values))
        exact = lax.Precision.HIGHEST
        narrow = jnp.concatenate(chunks, axis=0)
        grads = jnp.dot(
            narrow, ahead_ref[...], precision=exact, preferred_element_type=jnp.float32
        )
        fluxes = jnp.concatenate(
            [stacked(1) * grads[:, :LANES], stacked(2) * grads[:, LANES:]], axis=1
        )
        terms = jnp.dot(
            fluxes, back_ref[...], precision=exact, preferred_element_type=jnp.float32
        )
        grad = derivative(chunks, 0)
        grad = [geo_ref[0, :, c * LANES : (c + 1) * LANES] * grad[c] for c in range(4)]
        first = derivative(grad, 32)
        factor = factors[...]
        result = [
            terms[c * ELEMS : (c + 1) * ELEMS] + first[c] + factor * chunks[c] for c in range(4)
        ]
        for k in range(5):
            spread[pl.ds(k, ELEMS, stride=8), :] = pick(
                result, elem_inv[pl.ds(k, ELEMS, stride=8), :]
            )
        for e, row in enumerate(ROW_OF):
            sums[e % 3, row : row + 8, :] = spread[8 * e : 8 * e + 8, :]
        sums[0, 0:8, :] += pick([eight(last_row(r)) for r in result], wrap_inv[...])
        return sums[0] + sums[1] + sums[2]

    def dots(*products):
        lane = iota((1, LANES), 1)
        row = jnp.zeros((1, LANES), jnp.float32)
        for k, product in enumerate(products):
            total = jnp.sum(jnp.sum(product, axis=0, keepdims=True), axis=1, keepdims=True)
            row = jnp.where(lane == k, total, row)
        return row

    send[...] = jnp.zeros_like(send)
    spread[...] = jnp.zeros_like(spread)
    sums[...] = jnp.zeros_like(sums)
    resid[...] = jnp.zeros_like(resid)
    loads["lists"].wait()
    loads["rhs"].wait()
    for i in range(half):
        pair_up(
            list_idx,
            8 * i,
            lists_ref[:, i * LANES : (i + 1) * LANES],
            lists_ref[:, (i + half) * LANES : (i + half + 1) * LANES],
        )
    pair_up(
        list_idx,
        8 * half,
        lists_ref[:, FACE : FACE + DIAG],
        lists_ref[:, FACE + DIAG : FACE + 2 * DIAG],
    )
    for i in range(ROWS):
        resid[i : i + 1, :] = rhs_ref[:, i * LANES : (i + 1) * LANES]
    slot = iota((ROWS, LANES), 0) * LANES + iota((ROWS, LANES), 1)
    resid[0:ROWS, :] = jnp.where(slot < live * STRIDE, resid[0:ROWS, :], 0.0)
    fill_send(0, resid)
    pl.semaphore_wait(barrier, len(everyone))
    exchange = start_exchange(0)
    loads["order"].wait()
    loads["shift"].wait()
    set_up()
    same = iota((ELEMS, ELEMS), 0) == iota((ELEMS, ELEMS), 1)
    column = jnp.sum(jnp.where(same, shift_ref[...], 0.0), axis=1, keepdims=True)
    factors[...] = jnp.broadcast_to(column, (ELEMS, LANES))
    for name in ("ahead", "geo", "back", "coef"):
        loads[name].wait()
    for copy in exchange:
        copy.wait_recv()
    add_received(0, resid)

    part_w[...] = operate(resid)
    res0 = resid[...]
    summing = start_sum(0, 0, dots(res0 * res0 * inv_mult[...], res0 * part_w[...]))
    image[...] = part_w[...]
    fill_send(1, image)
    exchange = start_exchange(1)
    summing = start_sum(0, 1, end_sum(0, 0, summing))
    for copy in exchange:
        copy.wait_recv()
    add_received(1, image)

    second[...] = operate(image)
    fill_send(2, second)
    exchange = start_exchange(2)
    totals = end_sum(0, 1, summing)
    norm0 = totals[:, 0:1]
    energy0 = totals[:, 1:2]
    alpha0 = norm0 / energy0

    res0 = resid[...]
    image0 = image[...]
    res1 = res0 - alpha0 * image0
    scaled = res1 * inv_mult[...]
    row = dots(scaled * res1, res1 * (part_w[...] - alpha0 * second[...]), scaled * image0)
    summing = start_sum(1, 0, row)
    for copy in exchange:
        copy.wait_recv()
    add_received(2, second)
    earlier = list(copies)
    summing = start_sum(1, 1, end_sum(1, 0, summing))
    for copy in earlier:
        copy.wait_send()
    totals = end_sum(1, 1, summing)
    norm1 = totals[:, 0:1]
    beta = norm1 / norm0
    energy1 = totals[:, 1:2] + beta * (2.0 * totals[:, 2:3] + beta * energy0)
    alpha1 = norm1 / energy1

    res0 = resid[...]
    image0 = image[...]
    res1 = res0 - alpha0 * image0
    image1 = (image0 - alpha0 * second[...]) + beta * image0
    solved = alpha0 * res0 + alpha1 * (res1 + beta * res0)
    left = res1 - alpha1 * image1
    sol_ref[...] = solved[0:ROWS]
    res_ref[...] = left[0:ROWS]
    for copy in summing:
        copy.wait_send()


def solution(mesh):
    n_px = mesh.shape["px"]
    n_py = mesh.shape["py"]
    count = 3 * 8 + 2 * (n_px - 1 + n_py - 1)
    coef, ahead, back = tables()

    def body(right_side, geometry, shift, node_order, elem_counts, share_lists):
        vmem = pl.BlockSpec(memory_space=pltpu.VMEM)
        hbm = pl.BlockSpec(memory_space=pltpu.HBM)
        plane = jax.ShapeDtypeStruct((ROWS, LANES), jnp.float32)

        def stay(x):
            return pltpu.with_memory_space_constraint(x, pltpu.HBM)

        vector = pltpu.VMEM((PAD, LANES), jnp.float32)
        solved, left = pl.pallas_call(
            functools.partial(kernel, n_px, n_py),
            out_shape=(plane, plane),
            in_specs=[hbm] * 4 + [vmem] + [hbm] * 4,
            out_specs=(vmem, vmem),
            scratch_shapes=[
                pltpu.VMEM((1, ROWS * LANES), jnp.float32),
                pltpu.VMEM((3, ELEMS, 4 * LANES), jnp.float32),
                pltpu.VMEM((1, ELEMS), jnp.float32),
                pltpu.VMEM((ELEMS, 4 * LANES), jnp.int32),
                pltpu.VMEM((4, FACE + 2 * DIAG), jnp.int32),
                pltpu.VMEM(coef.shape, jnp.float32),
                pltpu.VMEM(ahead.shape, jnp.float32),
                pltpu.VMEM(back.shape, jnp.float32),
                pltpu.VMEM((ELEMS, LANES), jnp.float32),
                vector,
                vector,
                vector,
                vector,
                pltpu.VMEM((8 * ELEMS + 8, LANES), jnp.float32),
                pltpu.VMEM((8 * ELEMS + 8, LANES), jnp.float32),
                pltpu.VMEM((3, PAD, LANES), jnp.float32),
                pltpu.VMEM((8 * ELEMS + 8, LANES), jnp.int32),
                pltpu.VMEM((80, LANES), jnp.int32),
                pltpu.VMEM((8, LANES), jnp.int32),
                pltpu.VMEM((8, LANES), jnp.int32),
                vector,
                pltpu.VMEM((8, LANES), jnp.float32),
                pltpu.VMEM((8 * FACE_ROWS, LANES), jnp.float32),
                pltpu.VMEM((4 * FACE_ROWS + 8, LANES), jnp.int32),
                pltpu.VMEM((4 * FACE_ROWS, LANES), jnp.int32),
                pltpu.VMEM((8, 4 * LANES), jnp.int32),
                pltpu.VMEM((3 * TURN, LANES), jnp.float32),
                pltpu.VMEM((3 * TURN, LANES), jnp.float32),
                pltpu.VMEM((3 * 32, LANES), jnp.float32),
                pltpu.VMEM((2 * (n_px + n_py), 1, LANES), jnp.float32),
                pltpu.SemaphoreType.DMA((count,)),
                pltpu.SemaphoreType.DMA((count,)),
                pltpu.SemaphoreType.DMA((8,)),
            ],
            compiler_params=pltpu.CompilerParams(
                collective_id=0, has_side_effects=True, vmem_limit_bytes=32 * 2**20
            ),
            cost_estimate=pl.CostEstimate(
                flops=10**8, bytes_accessed=2 * 10**6, transcendentals=0
            ),
        )(
            stay(right_side[0]),
            stay(geometry[0, 0]),
            stay(shift[0]),
            stay(node_order[0, 0]),
            elem_counts,
            stay(share_lists[0, 0]),
            stay(jnp.asarray(coef)),
            stay(jnp.asarray(ahead)),
            stay(jnp.asarray(back)),
        )
        shape = (1, 1, ROWS * LANES)
        return solved.reshape(shape), left.reshape(shape)

    return jax.shard_map(
        body,
        mesh=mesh,
        in_specs=(
            P("px", "py", None),
            P("px", "py", None, None, None),
            P("px", "py", None),
            P("px", "py", None, None),
            P("px", "py"),
            P("px", "py", None, None),
        ),
        out_specs=(P("px", "py", None), P("px", "py", None)),
        check_vma=False,
    )
```

```python
import functools

import jax
import jax.numpy as jnp
import numpy as np
from jax import lax
from jax.experimental import pallas as pl
from jax.experimental.pallas import tpu as pltpu
from jax.sharding import PartitionSpec as P

STRIDE = 344
FACE = 1280
DIAG = 128
ELEMS = 48
LANES = 128
ROWS = 129
PAD = 136
FACE_ROWS = FACE // LANES
TURN = 80
ROW_OF = [e * STRIDE // LANES for e in range(ELEMS)]
LOWER = (1, 3, 2, 3)
UPPER = (0, 2, 0, 1)
FACE_STEPS = ((1, 0), (-1, 0), (0, 1), (0, -1))
DIAG_STEPS = ((1, 1), (1, -1), (-1, 1), (-1, -1))
DIAG_LIST = (0, 0, 1, 1)


def gll_derivative():
    degree = 7
    points = np.array(
        [
            -1.0,
            -0.8717401485096066,
            -0.5917001814331423,
            -0.2092992179024789,
            0.2092992179024789,
            0.5917001814331423,
            0.8717401485096066,
            1.0,
        ]
    )
    before = np.ones(8)
    current = points * 1.0
    for order in range(1, degree):
        following = ((2 * order + 1) * points * current - order * before) / (order + 1)
        before = current
        current = following
    same = np.arange(8)[:, None] == np.arange(8)[None, :]
    spacing = np.where(same, 1.0, points[:, None] - points[None, :])
    matrix = np.where(same, 0.0, current[:, None] / (current[None, :] * spacing))
    corner = np.array([-14.0, 0.0, 0.0, 0.0, 0.0, 0.0, 0.0, 14.0])
    return matrix + np.where(same, corner[:, None], 0.0)


def tables():
    deriv = gll_derivative()
    half = np.arange(LANES) // 64

    def lanes_of(matrix):
        rows = []
        for out in range(4):
            for src in range(4):
                rows.append(matrix[2 * out + half, 2 * src + half])
                rows.append(matrix[2 * out + half, 2 * src + 1 - half])
        return np.stack(rows)

    coef = np.concatenate([lanes_of(deriv), lanes_of(deriv.T)])
    second = np.kron(np.eye(2), np.kron(deriv, np.eye(8)))
    third = np.kron(np.eye(16), deriv)
    ahead = np.concatenate([second.T, third.T], axis=1)
    back = np.concatenate([second, third], axis=0)
    return tuple(np.asarray(t, np.float32) for t in (coef, ahead, back))


def take_lanes(values, lanes):
    return jnp.take_along_axis(values, lanes, axis=1, mode="promise_in_bounds")


def pick(sources, index):
    high = index >> 7
    lanes = index & 127
    total = None
    for j, source in enumerate(sources):
        found = take_lanes(source, lanes)
        total = jnp.where(high == j, found, 0.0 if total is None else total)
    return total


def eight(row):
    return jnp.broadcast_to(row, (8, row.shape[1]))


def iota(shape, dim):
    return lax.broadcasted_iota(jnp.int32, shape, dim)


def one_hot_lanes(low):
    return jnp.where(low == iota((LANES, low.shape[1]), 0), 1.0, 0.0).astype(jnp.bfloat16)


def over_lanes(left, right):
    return lax.dot_general(
        left, right, (((1,), (1,)), ((), ())), preferred_element_type=jnp.float32
    )


def inverse_rows(high, low, groups):
    count = high.shape[1]
    number = iota((groups, count), 1) + 1
    hit = high == iota((groups, count), 0)
    tens = jnp.where(hit, number >> 4, 0).astype(jnp.float32)
    ones = jnp.where(hit, number & 15, 0).astype(jnp.float32)
    left = jnp.concatenate([tens, ones], axis=0).astype(jnp.bfloat16)
    found = over_lanes(left, one_hot_lanes(low))
    return (16.0 * found[:groups] + found[groups:]).astype(jnp.int32) - 1


def kernel(
    n_px,
    n_py,
    rhs_hbm,
    geo_hbm,
    shift_hbm,
    order_hbm,
    count_ref,
    lists_hbm,
    coef_hbm,
    ahead_hbm,
    back_hbm,
    sol_ref,
    res_ref,
    rhs_ref,
    geo_ref,
    shift_ref,
    order_ref,
    lists_ref,
    coef_ref,
    ahead_ref,
    back_ref,
    factors,
    vec,
    parts,
    windows,
    spread,
    sums,
    elem_inv,
    face_inv,
    cross_inv,
    wrap_inv,
    inv_mult,
    cross_src,
    stack,
    list_idx,
    inv_idx,
    wrap_idx,
    send,
    recv,
    recv_diag,
    red,
    send_sem,
    recv_sem,
    load_sem,
):
    loads = {}
    for number, (name, src, dst) in enumerate(
        (
            ("lists", lists_hbm, lists_ref),
            ("rhs", rhs_hbm, rhs_ref),
            ("order", order_hbm, order_ref),
            ("shift", shift_hbm, shift_ref),
            ("ahead", ahead_hbm, ahead_ref),
            ("geo", geo_hbm, geo_ref),
            ("back", back_hbm, back_ref),
            ("coef", coef_hbm, coef_ref),
        )
    ):
        loads[name] = pltpu.make_async_copy(src, dst, load_sem.at[number])
        loads[name].start()

    px = lax.axis_index("px")
    py = lax.axis_index("py")

    def moved(step_x, step_y):
        return (lax.rem(px + step_x + n_px, n_px), lax.rem(py + step_y + n_py, n_py))

    sizes = (n_px, n_py)

    def place(stage):
        return px if stage == 0 else py

    def partner(stage, d):
        if stage == 0:
            return (lax.rem(px + d, n_px), py)
        return (px, lax.rem(py + d, n_py))

    def each_partner(stage, act):
        @pl.loop(1, sizes[stage])
        def _(d):
            act(d)

    barrier = pltpu.get_barrier_semaphore()

    def greet(other):
        pl.semaphore_signal(
            barrier, inc=1, device_id=other, device_id_type=pl.DeviceIdType.MESH
        )

    for step in FACE_STEPS + DIAG_STEPS:
        greet(moved(*step))
    for stage in range(2):
        each_partner(stage, lambda d, stage=stage: greet(partner(stage, d)))

    def remote(src, dst, number, other):
        return pltpu.make_async_remote_copy(
            src_ref=src,
            dst_ref=dst,
            send_sem=send_sem.at[number],
            recv_sem=recv_sem.at[number],
            device_id=other,
            device_id_type=pl.DeviceIdType.MESH,
        )

    def exchange(turn):
        copies = []
        for f, step in enumerate(FACE_STEPS):
            copies.append(
                remote(
                    send.at[turn, pl.ds(16 * f, 16)],
                    recv.at[turn, pl.ds(16 * (f ^ 1), 16)],
                    8 * turn + f,
                    moved(*step),
                )
            )
        for d, step in enumerate(DIAG_STEPS):
            copies.append(
                remote(
                    send.at[turn, pl.ds(16 * DIAG_LIST[d] + 8, 8)],
                    recv_diag.at[turn, pl.ds(8 * (3 - d), 8)],
                    8 * turn + 4 + d,
                    moved(*step),
                )
            )
        return copies

    def sum_copy(turn, stage, d):
        mine = turn * (n_px + n_py) + stage * n_px + place(stage)
        number = 24 + turn * (n_px + n_py - 2) + stage * (n_px - 1) + d - 1
        return remote(red.at[mine], red.at[mine], number, partner(stage, d))

    def start_sum(turn, stage, row):
        mine = turn * (n_px + n_py) + stage * n_px + place(stage)
        red[pl.ds(mine, 1)] = row[None]
        each_partner(stage, lambda d: sum_copy(turn, stage, d).start())

    def end_sum(turn, stage):
        each_partner(stage, lambda d: sum_copy(turn, stage, d).wait_recv())
        first = turn * (n_px + n_py) + stage * n_px
        rows = [red[first + slot] for slot in range(sizes[stage])]
        while len(rows) > 1:
            rows = [x + y for x, y in zip(rows[::2], rows[1::2])]
        return rows[0]

    def sum_left(turn, stage):
        each_partner(stage, lambda d: sum_copy(turn, stage, d).wait_send())

    live = count_ref[...]

    half = FACE_ROWS // 2

    def pair_up(target, at, upper, lower):
        target[at : at + 4, :] = upper
        target[at + 4 : at + 8, :] = lower

    def stack_rows(source, step):
        for j in range(FACE_ROWS):
            rows = source[pl.ds(j, 4, stride=step), :]
            pair_up(stack, 8 * j, rows, rows)
        return [stack[8 * j : 8 * j + 8, :] for j in range(FACE_ROWS)]

    def fill_send(turn, source):
        rows = stack_rows(source, FACE_ROWS)
        for i in range(half):
            found = pick(rows, list_idx[8 * i : 8 * i + 8, :])
            send[turn, pl.ds(i, 4, stride=16), :] = found[0:4]
            send[turn, pl.ds(i + half, 4, stride=16), :] = found[4:8]
        first = 4 * FACE_ROWS
        for at, q in enumerate(LOWER + UPPER):
            cross_src[at : at + 1, :] = source[first + q : first + q + 1, :]
        found = pick([cross_src[...]], list_idx[8 * half : 8 * half + 8, :])
        send[turn, pl.ds(FACE_ROWS, 4, stride=16), :] = found[0:4]
        send[turn, pl.ds(FACE_ROWS + 1, 4, stride=16), :] = found[4:8]

    def add_received(turn, target):
        rows = stack_rows(recv.at[turn], 16)
        for i in range(half):
            found = pick(rows, inv_idx[8 * i : 8 * i + 8, :])
            target[pl.ds(i, 4, stride=FACE_ROWS), :] += found[0:4]
            target[pl.ds(i + half, 4, stride=FACE_ROWS), :] += found[4:8]
        for part in range(2):
            rows = recv[turn, pl.ds(FACE_ROWS + part, 4, stride=16), :]
            cross_src[4 * part : 4 * part + 4, :] = rows
        for row, q, i in ((2, 2, 2), (3, 3, 3), (6, 0, 2), (7, 1, 3)):
            at = 8 * q + i
            cross_src[row : row + 1, :] += recv_diag[turn, at : at + 1, :]
        found = pick([cross_src[...]], cross_inv[...])
        first = 4 * FACE_ROWS
        for at, q in enumerate(LOWER + UPPER):
            target[first + q : first + q + 1, :] += found[at : at + 1]

    element = iota((ELEMS, LANES), 0)
    offset = (element * STRIDE) & 127
    is_last = element == live - 1

    def orders(c):
        return order_ref[:, c * LANES : (c + 1) * LANES]

    def last_row(values):
        return jnp.sum(jnp.where(is_last, values, jnp.zeros_like(values)), axis=0, keepdims=True)

    def set_up():
        for f in range(4):
            row = lists_ref[f : f + 1, 0:FACE]
            face_inv[16 * f : 16 * f + 16, :] = inverse_rows(row >> 7, row & 127, 16)
            for part in range(2):
                at = FACE + part * DIAG
                row = lists_ref[f : f + 1, at : at + DIAG]
                number = (iota((8, DIAG), 1) + 1).astype(jnp.float32).astype(jnp.bfloat16)
                found = over_lanes(number, one_hot_lanes(row))
                cross_inv[4 * part + f : 4 * part + f + 1, :] = found[0:1].astype(jnp.int32) - 1
        for i in range(half):
            pair_up(
                inv_idx,
                8 * i,
                face_inv[pl.ds(i, 4, stride=16), :],
                face_inv[pl.ds(i + half, 4, stride=16), :],
            )
        inv_mult[...] = jnp.ones_like(inv_mult)
        for f in range(4):
            named = face_inv[16 * f : 16 * f + FACE_ROWS, :] >= 0
            inv_mult[f * FACE_ROWS : (f + 1) * FACE_ROWS, :] = jnp.where(named, 0.5, 1.0)
        for q in range(4):
            copies_of = jnp.ones((1, LANES), jnp.float32)
            for part, regions in enumerate((LOWER, UPPER)):
                for f, region in enumerate(regions):
                    if region == q:
                        row = cross_inv[4 * part + f : 4 * part + f + 1, :]
                        copies_of = copies_of + jnp.where(row >= 0, 1.5, 0.0)
            at = 4 * FACE_ROWS + q
            inv_mult[at : at + 1, :] = 1.0 / copies_of

        @pl.loop(0, ELEMS // 8)
        def _(group):
            block = order_ref[pl.ds(pl.multiple_of(8 * group, 8), 8), :]
            for s in range(8):
                e = 8 * group + s
                row = block[s : s + 1]
                shifted = row + lax.rem(e * STRIDE, LANES)
                own = jnp.where(live <= e, 0, jnp.where(live == e + 1, STRIDE, 4 * LANES))
                high = jnp.where(row >= own, 7, shifted >> 7)
                elem_inv[pl.ds(pl.multiple_of(8 * e, 8), 8), :] = inverse_rows(
                    high, shifted & 127, 8
                )

        wrapped = jnp.concatenate([last_row(orders(c)) for c in range(4)], axis=1) - STRIDE
        wrap_inv[...] = inverse_rows(wrapped >> 7, wrapped & 127, 8)
        wrap_idx[...] = eight(wrapped)

    def derivative(chunks, first):
        swapped = [pltpu.roll(u, 64, 1) for u in chunks]
        result = []
        for out in range(4):
            total = None
            for src in range(4):
                at = first + (out * 4 + src) * 2
                term = coef_ref[at : at + 1, :] * chunks[src]
                total = term if total is None else total + term
                total = total + coef_ref[at + 1 : at + 2, :] * swapped[src]
            result.append(total)
        return result

    def stacked(k):
        return jnp.concatenate(
            [geo_ref[k, :, c * LANES : (c + 1) * LANES] for c in range(4)], axis=0
        )

    def operate(source):
        for e, row in enumerate(ROW_OF):
            windows[8 * e : 8 * e + 8, :] = source[row : row + 8, :]
        rows = [windows[pl.ds(k, ELEMS, stride=8), :] for k in range(5)]
        chunks = []
        for c in range(4):
            order = orders(c)
            around = pick(
                [eight(source[0:1, :]), eight(source[1:2, :])],
                wrap_idx[:, c * LANES : (c + 1) * LANES],
            )[0:1]
            values = pick(rows, order + offset)
            chunks.append(jnp.where(is_last & (order >= STRIDE), around, values))
        exact = lax.Precision.HIGHEST
        narrow = jnp.concatenate(chunks, axis=0)
        grads = jnp.dot(
            narrow, ahead_ref[...], precision=exact, preferred_element_type=jnp.float32
        )
        fluxes = jnp.concatenate(
            [stacked(1) * grads[:, :LANES], stacked(2) * grads[:, LANES:]], axis=1
        )
        terms = jnp.dot(
            fluxes, back_ref[...], precision=exact, preferred_element_type=jnp.float32
        )
        grad = derivative(chunks, 0)
        grad = [geo_ref[0, :, c * LANES : (c + 1) * LANES] * grad[c] for c in range(4)]
        first = derivative(grad, 32)
        factor = factors[...]
        result = [
            terms[c * ELEMS : (c + 1) * ELEMS] + first[c] + factor * chunks[c] for c in range(4)
        ]
        for k in range(5):
            spread[pl.ds(k, ELEMS, stride=8), :] = pick(
                result, elem_inv[pl.ds(k, ELEMS, stride=8), :]
            )
        for e, row in enumerate(ROW_OF):
            sums[e % 3, row : row + 8, :] = spread[8 * e : 8 * e + 8, :]
        sums[0, 0:8, :] += pick([eight(last_row(r)) for r in result], wrap_inv[...])
        return sums[0] + sums[1] + sums[2]

    def dots(*products):
        lane = iota((1, LANES), 1)
        row = jnp.zeros((1, LANES), jnp.float32)
        for k, product in enumerate(products):
            total = jnp.sum(jnp.sum(product, axis=0, keepdims=True), axis=1, keepdims=True)
            row = jnp.where(lane == k, total, row)
        return row

    send[...] = jnp.zeros_like(send)
    spread[...] = jnp.zeros_like(spread)
    sums[...] = jnp.zeros_like(sums)
    resid, image, second = (vec.at[k] for k in range(3))
    resid[...] = jnp.zeros((PAD, LANES), jnp.float32)
    loads["lists"].wait()
    loads["rhs"].wait()
    for i in range(half):
        pair_up(
            list_idx,
            8 * i,
            lists_ref[:, i * LANES : (i + 1) * LANES],
            lists_ref[:, (i + half) * LANES : (i + half + 1) * LANES],
        )
    pair_up(
        list_idx,
        8 * half,
        lists_ref[:, FACE : FACE + DIAG],
        lists_ref[:, FACE + DIAG : FACE + 2 * DIAG],
    )
    for i in range(ROWS):
        resid[i : i + 1, :] = rhs_ref[:, i * LANES : (i + 1) * LANES]
    slot = iota((ROWS, LANES), 0) * LANES + iota((ROWS, LANES), 1)
    resid[0:ROWS, :] = jnp.where(slot < live * STRIDE, resid[0:ROWS, :], 0.0)
    fill_send(0, resid)
    pl.semaphore_wait(barrier, 8 + (n_px - 1) + (n_py - 1))
    for copy in exchange(0):
        copy.start()
    loads["order"].wait()
    loads["shift"].wait()
    set_up()
    same = iota((ELEMS, ELEMS), 0) == iota((ELEMS, ELEMS), 1)
    column = jnp.sum(jnp.where(same, shift_ref[...], 0.0), axis=1, keepdims=True)
    factors[...] = jnp.broadcast_to(column, (ELEMS, LANES))
    for name in ("ahead", "geo", "back", "coef"):
        loads[name].wait()

    @pl.loop(0, 2)
    def _(turn):
        for copy in exchange(turn):
            copy.wait_recv()
        add_received(turn, vec.at[turn])
        terms = operate(vec.at[turn])
        vec[turn + 1] = terms
        parts[turn] = terms

        @pl.when(turn == 0)
        def _():
            res0 = resid[...]
            start_sum(0, 0, dots(res0 * res0 * inv_mult[...], res0 * parts[0]))

        fill_send(turn + 1, vec.at[turn + 1])
        for copy in exchange(turn + 1):
            copy.start()

        @pl.when(turn == 0)
        def _():
            start_sum(0, 1, end_sum(0, 0))

    totals = end_sum(0, 1)
    norm0 = totals[:, 0:1]
    energy0 = totals[:, 1:2]
    alpha0 = norm0 / energy0

    res0 = resid[...]
    image0 = image[...]
    res1 = res0 - alpha0 * image0
    scaled = res1 * inv_mult[...]
    row = dots(scaled * res1, res1 * (parts[0] - alpha0 * parts[1]), scaled * image0)
    start_sum(1, 0, row)
    for copy in exchange(2):
        copy.wait_recv()
    add_received(2, second)
    start_sum(1, 1, end_sum(1, 0))
    for turn in range(3):
        for copy in exchange(turn):
            copy.wait_send()
    for turn, stage in ((0, 0), (0, 1), (1, 0)):
        sum_left(turn, stage)
    totals = end_sum(1, 1)
    norm1 = totals[:, 0:1]
    beta = norm1 / norm0
    energy1 = totals[:, 1:2] + beta * (2.0 * totals[:, 2:3] + beta * energy0)
    alpha1 = norm1 / energy1

    res0 = resid[...]
    image0 = image[...]
    res1 = res0 - alpha0 * image0
    image1 = (image0 - alpha0 * second[...]) + beta * image0
    solved = alpha0 * res0 + alpha1 * (res1 + beta * res0)
    left = res1 - alpha1 * image1
    sol_ref[...] = solved[0:ROWS]
    res_ref[...] = left[0:ROWS]
    sum_left(1, 1)


def solution(mesh):
    n_px = mesh.shape["px"]
    n_py = mesh.shape["py"]
    count = 3 * 8 + 2 * (n_px - 1 + n_py - 1)
    coef, ahead, back = tables()

    def body(right_side, geometry, shift, node_order, elem_counts, share_lists):
        vmem = pl.BlockSpec(memory_space=pltpu.VMEM)
        hbm = pl.BlockSpec(memory_space=pltpu.HBM)
        plane = jax.ShapeDtypeStruct((ROWS, LANES), jnp.float32)

        def stay(x):
            return pltpu.with_memory_space_constraint(x, pltpu.HBM)

        vector = pltpu.VMEM((PAD, LANES), jnp.float32)
        solved, left = pl.pallas_call(
            functools.partial(kernel, n_px, n_py),
            out_shape=(plane, plane),
            in_specs=[hbm] * 4 + [vmem] + [hbm] * 4,
            out_specs=(vmem, vmem),
            scratch_shapes=[
                pltpu.VMEM((1, ROWS * LANES), jnp.float32),
                pltpu.VMEM((3, ELEMS, 4 * LANES), jnp.float32),
                pltpu.VMEM((1, ELEMS), jnp.float32),
                pltpu.VMEM((ELEMS, 4 * LANES), jnp.int32),
                pltpu.VMEM((4, FACE + 2 * DIAG), jnp.int32),
                pltpu.VMEM(coef.shape, jnp.float32),
                pltpu.VMEM(ahead.shape, jnp.float32),
                pltpu.VMEM(back.shape, jnp.float32),
                pltpu.VMEM((ELEMS, LANES), jnp.float32),
                pltpu.VMEM((3, PAD, LANES), jnp.float32),
                pltpu.VMEM((2, PAD, LANES), jnp.float32),
                pltpu.VMEM((8 * ELEMS + 8, LANES), jnp.float32),
                pltpu.VMEM((8 * ELEMS + 8, LANES), jnp.float32),
                pltpu.VMEM((3, PAD, LANES), jnp.float32),
                pltpu.VMEM((8 * ELEMS + 8, LANES), jnp.int32),
                pltpu.VMEM((80, LANES), jnp.int32),
                pltpu.VMEM((8, LANES), jnp.int32),
                pltpu.VMEM((8, LANES), jnp.int32),
                vector,
                pltpu.VMEM((8, LANES), jnp.float32),
                pltpu.VMEM((8 * FACE_ROWS, LANES), jnp.float32),
                pltpu.VMEM((4 * FACE_ROWS + 8, LANES), jnp.int32),
                pltpu.VMEM((4 * FACE_ROWS, LANES), jnp.int32),
                pltpu.VMEM((8, 4 * LANES), jnp.int32),
                pltpu.VMEM((3, TURN, LANES), jnp.float32),
                pltpu.VMEM((3, TURN, LANES), jnp.float32),
                pltpu.VMEM((3, 32, LANES), jnp.float32),
                pltpu.VMEM((2 * (n_px + n_py), 1, LANES), jnp.float32),
                pltpu.SemaphoreType.DMA((count,)),
                pltpu.SemaphoreType.DMA((count,)),
                pltpu.SemaphoreType.DMA((8,)),
            ],
            compiler_params=pltpu.CompilerParams(
                collective_id=0, has_side_effects=True, vmem_limit_bytes=32 * 2**20
            ),
            cost_estimate=pl.CostEstimate(
                flops=10**8, bytes_accessed=2 * 10**6, transcendentals=0
            ),
        )(
            stay(right_side[0]),
            stay(geometry[0, 0]),
            stay(shift[0]),
            stay(node_order[0, 0]),
            elem_counts,
            stay(share_lists[0, 0]),
            stay(jnp.asarray(coef)),
            stay(jnp.asarray(ahead)),
            stay(jnp.asarray(back)),
        )
        shape = (1, 1, ROWS * LANES)
        return solved.reshape(shape), left.reshape(shape)

    return jax.shard_map(
        body,
        mesh=mesh,
        in_specs=(
            P("px", "py", None),
            P("px", "py", None, None, None),
            P("px", "py", None),
            P("px", "py", None, None),
            P("px", "py"),
            P("px", "py", None, None),
        ),
        out_specs=(P("px", "py", None), P("px", "py", None)),
        check_vma=False,
    )
```

```python
import functools

import jax
import jax.numpy as jnp
import numpy as np
from jax import lax
from jax.experimental import pallas as pl
from jax.experimental.pallas import tpu as pltpu
from jax.sharding import PartitionSpec as P

STRIDE = 344
FACE = 1280
DIAG = 128
ELEMS = 48
LANES = 128
ROWS = 129
PAD = 136
FACE_ROWS = FACE // LANES
TURN = 80
SCALE = 2.0**-16
ROW_OF = [e * STRIDE // LANES for e in range(ELEMS)]
LOWER = (1, 3, 2, 3)
UPPER = (0, 2, 0, 1)
FACE_STEPS = ((1, 0), (-1, 0), (0, 1), (0, -1))
DIAG_STEPS = ((1, 1), (1, -1), (-1, 1), (-1, -1))
DIAG_LIST = (0, 0, 1, 1)


def gll_derivative():
    degree = 7
    points = np.array(
        [
            -1.0,
            -0.8717401485096066,
            -0.5917001814331423,
            -0.2092992179024789,
            0.2092992179024789,
            0.5917001814331423,
            0.8717401485096066,
            1.0,
        ]
    )
    before = np.ones(8)
    current = points * 1.0
    for order in range(1, degree):
        following = ((2 * order + 1) * points * current - order * before) / (order + 1)
        before = current
        current = following
    same = np.arange(8)[:, None] == np.arange(8)[None, :]
    spacing = np.where(same, 1.0, points[:, None] - points[None, :])
    matrix = np.where(same, 0.0, current[:, None] / (current[None, :] * spacing))
    corner = np.array([-14.0, 0.0, 0.0, 0.0, 0.0, 0.0, 0.0, 14.0])
    return matrix + np.where(same, corner[:, None], 0.0)


def tables():
    deriv = gll_derivative()
    half = np.arange(LANES) // 64

    def lanes_of(matrix):
        rows = []
        for out in range(4):
            for src in range(4):
                rows.append(matrix[2 * out + half, 2 * src + half])
                rows.append(matrix[2 * out + half, 2 * src + 1 - half])
        return np.stack(rows)

    coef = np.concatenate([lanes_of(deriv), SCALE * lanes_of(deriv.T)])
    second = np.kron(np.eye(2), np.kron(deriv, np.eye(8)))
    third = np.kron(np.eye(16), deriv)
    ahead = np.concatenate([second.T, third.T], axis=1)
    back = SCALE * np.concatenate([second, third], axis=0)
    return tuple(np.asarray(t, np.float32) for t in (coef, ahead, back))


def take_lanes(values, lanes):
    return jnp.take_along_axis(values, lanes, axis=1, mode="promise_in_bounds")


def pick(sources, index):
    high = index >> 7
    lanes = index & 127
    total = None
    for j, source in enumerate(sources):
        found = take_lanes(source, lanes)
        total = jnp.where(high == j, found, 0.0 if total is None else total)
    return total


def sum_exactly(rows):
    errors = []
    while len(rows) > 1:
        sums_of = []
        for x, y in zip(rows[::2], rows[1::2]):
            total = x + y
            part = total - x
            errors.append((x - (total - part)) + (y - part))
            sums_of.append(total)
        rows = sums_of
    while len(errors) > 1:
        odd = errors[len(errors) // 2 * 2 :]
        errors = [x + y for x, y in zip(errors[::2], errors[1::2])] + odd
    return rows[0], errors[0]


def split(x):
    small = x * 2.0**-16
    wide = small * 4097.0
    high = (wide - (wide - small)) * 2.0**16
    return high, x - high


def product_less(factor, times, less):
    product = factor * times[0]
    (f_high, f_low), (t_high, t_low) = split(factor), split(times[0])
    error = ((f_high * t_high - product) + f_high * t_low + f_low * t_high) + f_low * t_low
    return (product - less[0]) + ((error - less[1]) + factor * times[1])


def eight(row):
    return jnp.broadcast_to(row, (8, row.shape[1]))


def iota(shape, dim):
    return lax.broadcasted_iota(jnp.int32, shape, dim)


def one_hot_lanes(low):
    return jnp.where(low == iota((LANES, low.shape[1]), 0), 1.0, 0.0).astype(jnp.bfloat16)


def over_lanes(left, right):
    return lax.dot_general(
        left, right, (((1,), (1,)), ((), ())), preferred_element_type=jnp.float32
    )


def inverse_rows(high, low, groups):
    count = high.shape[1]
    number = iota((groups, count), 1) + 1
    hit = high == iota((groups, count), 0)
    tens = jnp.where(hit, number >> 4, 0).astype(jnp.float32)
    ones = jnp.where(hit, number & 15, 0).astype(jnp.float32)
    left = jnp.concatenate([tens, ones], axis=0).astype(jnp.bfloat16)
    found = over_lanes(left, one_hot_lanes(low))
    return (16.0 * found[:groups] + found[groups:]).astype(jnp.int32) - 1


def kernel(
    n_px,
    n_py,
    rhs_hbm,
    geo_hbm,
    shift_hbm,
    order_hbm,
    count_ref,
    lists_hbm,
    coef_hbm,
    ahead_hbm,
    back_hbm,
    sol_ref,
    res_ref,
    rhs_ref,
    geo_ref,
    shift_ref,
    order_ref,
    lists_ref,
    coef_ref,
    ahead_ref,
    back_ref,
    factors,
    resid,
    image,
    second,
    part,
    windows,
    spread,
    sums,
    elem_inv,
    face_inv,
    cross_inv,
    wrap_inv,
    inv_mult,
    cross_src,
    stack,
    list_idx,
    inv_idx,
    wrap_idx,
    send,
    recv,
    recv_diag,
    red,
    send_sem,
    recv_sem,
    load_sem,
):
    loads = {}
    for number, (name, src, dst) in enumerate(
        (
            ("lists", lists_hbm, lists_ref),
            ("rhs", rhs_hbm, rhs_ref),
            ("order", order_hbm, order_ref),
            ("shift", shift_hbm, shift_ref),
            ("ahead", ahead_hbm, ahead_ref),
            ("geo", geo_hbm, geo_ref),
            ("back", back_hbm, back_ref),
            ("coef", coef_hbm, coef_ref),
        )
    ):
        loads[name] = pltpu.make_async_copy(src, dst, load_sem.at[number])
        loads[name].start()

    px = lax.axis_index("px")
    py = lax.axis_index("py")

    def moved(step_x, step_y):
        return (lax.rem(px + step_x + n_px, n_px), lax.rem(py + step_y + n_py, n_py))

    sizes = (n_px, n_py)

    def place(stage):
        return px if stage == 0 else py

    def partners(stage):
        if stage == 0:
            return [(lax.rem(px + d, n_px), py) for d in range(1, n_px)]
        return [(px, lax.rem(py + d, n_py)) for d in range(1, n_py)]

    everyone = [moved(*step) for step in FACE_STEPS + DIAG_STEPS]
    everyone += partners(0) + partners(1)
    barrier = pltpu.get_barrier_semaphore()
    for other in everyone:
        pl.semaphore_signal(
            barrier, inc=1, device_id=other, device_id_type=pl.DeviceIdType.MESH
        )

    copies = []

    def start_copy(src, dst, other):
        number = len(copies)
        copy = pltpu.make_async_remote_copy(
            src_ref=src,
            dst_ref=dst,
            send_sem=send_sem.at[number],
            recv_sem=recv_sem.at[number],
            device_id=other,
            device_id_type=pl.DeviceIdType.MESH,
        )
        copy.start()
        copies.append(copy)
        return copy

    def start_exchange(turn):
        started = []
        for f, step in enumerate(FACE_STEPS):
            started.append(
                start_copy(
                    send.at[pl.ds(TURN * turn + 16 * f, 16)],
                    recv.at[pl.ds(TURN * turn + 16 * (f ^ 1), 16)],
                    moved(*step),
                )
            )
        for d, step in enumerate(DIAG_STEPS):
            started.append(
                start_copy(
                    send.at[pl.ds(TURN * turn + 16 * DIAG_LIST[d] + 8, 8)],
                    recv_diag.at[pl.ds(32 * turn + 8 * (3 - d), 8)],
                    moved(*step),
                )
            )
        return started

    def start_sum(stage, row):
        mine = stage * n_px + place(stage)
        red[pl.ds(mine, 1)] = row[None]
        return [start_copy(red.at[mine], red.at[mine], other) for other in partners(stage)]

    def end_sum(stage, started):
        for copy in started:
            copy.wait_recv()
        return sum_exactly([red[stage * n_px + slot] for slot in range(sizes[stage])])

    live = count_ref[...]

    half = FACE_ROWS // 2

    def pair_up(target, at, upper, lower):
        target[at : at + 4, :] = upper
        target[at + 4 : at + 8, :] = lower

    def stack_rows(source, first, step):
        for j in range(FACE_ROWS):
            rows = source[pl.ds(first + j, 4, stride=step), :]
            pair_up(stack, 8 * j, rows, rows)
        return [stack[8 * j : 8 * j + 8, :] for j in range(FACE_ROWS)]

    def fill_send(turn, source):
        rows = stack_rows(source, 0, FACE_ROWS)
        for i in range(half):
            found = pick(rows, list_idx[8 * i : 8 * i + 8, :])
            send[pl.ds(TURN * turn + i, 4, stride=16), :] = found[0:4]
            send[pl.ds(TURN * turn + i + half, 4, stride=16), :] = found[4:8]
        first = 4 * FACE_ROWS
        for at, q in enumerate(LOWER + UPPER):
            cross_src[at : at + 1, :] = source[first + q : first + q + 1, :]
        found = pick([cross_src[...]], list_idx[8 * half : 8 * half + 8, :])
        send[pl.ds(TURN * turn + FACE_ROWS, 4, stride=16), :] = found[0:4]
        send[pl.ds(TURN * turn + FACE_ROWS + 1, 4, stride=16), :] = found[4:8]

    def add_received(turn, target):
        rows = stack_rows(recv, TURN * turn, 16)
        for i in range(half):
            found = pick(rows, inv_idx[8 * i : 8 * i + 8, :])
            target[pl.ds(i, 4, stride=FACE_ROWS), :] += found[0:4]
            target[pl.ds(i + half, 4, stride=FACE_ROWS), :] += found[4:8]
        for part in range(2):
            at = TURN * turn + FACE_ROWS + part
            cross_src[4 * part : 4 * part + 4, :] = recv[pl.ds(at, 4, stride=16), :]
        for row, q, i in ((2, 2, 2), (3, 3, 3), (6, 0, 2), (7, 1, 3)):
            at = 32 * turn + 8 * q + i
            cross_src[row : row + 1, :] += recv_diag[at : at + 1, :]
        found = pick([cross_src[...]], cross_inv[...])
        first = 4 * FACE_ROWS
        for at, q in enumerate(LOWER + UPPER):
            target[first + q : first + q + 1, :] += found[at : at + 1]

    element = iota((ELEMS, LANES), 0)
    offset = (element * STRIDE) & 127
    is_last = element == live - 1

    def orders(c):
        return order_ref[:, c * LANES : (c + 1) * LANES]

    def last_row(values):
        return jnp.sum(jnp.where(is_last, values, jnp.zeros_like(values)), axis=0, keepdims=True)

    def set_up():
        for f in range(4):
            row = lists_ref[f : f + 1, 0:FACE]
            face_inv[16 * f : 16 * f + 16, :] = inverse_rows(row >> 7, row & 127, 16)
            for part in range(2):
                at = FACE + part * DIAG
                row = lists_ref[f : f + 1, at : at + DIAG]
                number = (iota((8, DIAG), 1) + 1).astype(jnp.float32).astype(jnp.bfloat16)
                found = over_lanes(number, one_hot_lanes(row))
                cross_inv[4 * part + f : 4 * part + f + 1, :] = found[0:1].astype(jnp.int32) - 1
        for i in range(half):
            pair_up(
                inv_idx,
                8 * i,
                face_inv[pl.ds(i, 4, stride=16), :],
                face_inv[pl.ds(i + half, 4, stride=16), :],
            )
        inv_mult[...] = jnp.ones_like(inv_mult)
        for f in range(4):
            named = face_inv[16 * f : 16 * f + FACE_ROWS, :] >= 0
            inv_mult[f * FACE_ROWS : (f + 1) * FACE_ROWS, :] = jnp.where(named, 0.5, 1.0)
        for q in range(4):
            copies_of = jnp.ones((1, LANES), jnp.float32)
            for part, regions in enumerate((LOWER, UPPER)):
                for f, region in enumerate(regions):
                    if region == q:
                        row = cross_inv[4 * part + f : 4 * part + f + 1, :]
                        copies_of = copies_of + jnp.where(row >= 0, 1.5, 0.0)
            at = 4 * FACE_ROWS + q
            inv_mult[at : at + 1, :] = 1.0 / copies_of

        @pl.loop(0, ELEMS // 8)
        def _(group):
            block = order_ref[pl.ds(pl.multiple_of(8 * group, 8), 8), :]
            for s in range(8):
                e = 8 * group + s
                row = block[s : s + 1]
                shifted = row + lax.rem(e * STRIDE, LANES)
                own = jnp.where(live <= e, 0, jnp.where(live == e + 1, STRIDE, 4 * LANES))
                high = jnp.where(row >= own, 7, shifted >> 7)
                elem_inv[pl.ds(pl.multiple_of(8 * e, 8), 8), :] = inverse_rows(
                    high, shifted & 127, 8
                )

        wrapped = jnp.concatenate([last_row(orders(c)) for c in range(4)], axis=1) - STRIDE
        wrap_inv[...] = inverse_rows(wrapped >> 7, wrapped & 127, 8)
        wrap_idx[...] = eight(wrapped)

    def derivative(chunks, first):
        swapped = [pltpu.roll(u, 64, 1) for u in chunks]
        result = []
        for out in range(4):
            total = None
            for src in range(4):
                at = first + (out * 4 + src) * 2
                term = coef_ref[at : at + 1, :] * chunks[src]
                total = term if total is None else total + term
                total = total + coef_ref[at + 1 : at + 2, :] * swapped[src]
            result.append(total)
        return result

    def stacked(k):
        return jnp.concatenate(
            [geo_ref[k, :, c * LANES : (c + 1) * LANES] for c in range(4)], axis=0
        )

    def operate(source):
        for e, row in enumerate(ROW_OF):
            windows[8 * e : 8 * e + 8, :] = source[row : row + 8, :]
        rows = [windows[pl.ds(k, ELEMS, stride=8), :] for k in range(5)]
        chunks = []
        for c in range(4):
            order = orders(c)
            around = pick(
                [eight(source[0:1, :]), eight(source[1:2, :])],
                wrap_idx[:, c * LANES : (c + 1) * LANES],
            )[0:1]
            values = pick(rows, order + offset)
            chunks.append(jnp.where(is_last & (order >= STRIDE), around, values))
        exact = lax.Precision.HIGHEST
        narrow = jnp.concatenate(chunks, axis=0)
        grads = jnp.dot(
            narrow, ahead_ref[...], precision=exact, preferred_element_type=jnp.float32
        )
        fluxes = jnp.concatenate(
            [stacked(1) * grads[:, :LANES], stacked(2) * grads[:, LANES:]], axis=1
        )
        terms = jnp.dot(
            fluxes, back_ref[...], precision=exact, preferred_element_type=jnp.float32
        )
        grad = derivative(chunks, 0)
        grad = [geo_ref[0, :, c * LANES : (c + 1) * LANES] * grad[c] for c in range(4)]
        first = derivative(grad, 32)
        factor = factors[...]
        result = [
            terms[c * ELEMS : (c + 1) * ELEMS] + first[c] + factor * chunks[c] for c in range(4)
        ]
        for k in range(5):
            spread[pl.ds(k, ELEMS, stride=8), :] = pick(
                result, elem_inv[pl.ds(k, ELEMS, stride=8), :]
            )
        for e, row in enumerate(ROW_OF):
            sums[e % 3, row : row + 8, :] = spread[8 * e : 8 * e + 8, :]
        sums[0, 0:8, :] += pick([eight(last_row(r)) for r in result], wrap_inv[...])
        return sums[0] + sums[1] + sums[2]

    lane = iota((1, LANES), 1)

    def dots(first, row, *products):
        for k, product in enumerate(products, first):
            total = jnp.sum(jnp.sum(product, axis=0, keepdims=True), axis=1, keepdims=True)
            row = jnp.where(lane == k, total, row)
        return row

    send[...] = jnp.zeros_like(send)
    spread[...] = jnp.zeros_like(spread)
    sums[...] = jnp.zeros_like(sums)
    resid[...] = jnp.zeros_like(resid)
    loads["lists"].wait()
    loads["rhs"].wait()
    for i in range(half):
        pair_up(
            list_idx,
            8 * i,
            lists_ref[:, i * LANES : (i + 1) * LANES],
            lists_ref[:, (i + half) * LANES : (i + half + 1) * LANES],
        )
    pair_up(
        list_idx,
        8 * half,
        lists_ref[:, FACE : FACE + DIAG],
        lists_ref[:, FACE + DIAG : FACE + 2 * DIAG],
    )
    for i in range(ROWS):
        resid[i : i + 1, :] = rhs_ref[:, i * LANES : (i + 1) * LANES]
    slot = iota((ROWS, LANES), 0) * LANES + iota((ROWS, LANES), 1)
    resid[0:ROWS, :] = jnp.where(slot < live * STRIDE, resid[0:ROWS, :], 0.0)
    fill_send(0, resid)
    pl.semaphore_wait(barrier, len(everyone))
    exchange = start_exchange(0)
    loads["order"].wait()
    loads["shift"].wait()
    set_up()
    same = iota((ELEMS, ELEMS), 0) == iota((ELEMS, ELEMS), 1)
    column = jnp.sum(jnp.where(same, shift_ref[...], 0.0), axis=1, keepdims=True)
    factors[...] = jnp.broadcast_to(SCALE * column, (ELEMS, LANES))
    for name in ("ahead", "geo", "back", "coef"):
        loads[name].wait()
    for copy in exchange:
        copy.wait_recv()
    add_received(0, resid)

    part[...] = operate(resid)
    image[...] = part[...]
    fill_send(1, image)
    exchange = start_exchange(1)
    res0 = resid[...]
    row = jnp.zeros((1, LANES), jnp.float32)
    row = dots(0, row, res0 * res0 * inv_mult[...], res0 * part[...])
    for copy in exchange:
        copy.wait_recv()
    add_received(1, image)

    part[...] = operate(image)
    image0 = image[...]
    row = dots(2, row, image0 * image0 * inv_mult[...], image0 * part[...])
    summing = start_sum(0, row)
    second[...] = part[...]
    fill_send(2, second)
    exchange = start_exchange(2)
    total, rest = end_sum(0, summing)
    summing = start_sum(1, jnp.where(lane < 64, total, pltpu.roll(rest, 64, 1)))
    for copy in exchange:
        copy.wait_recv()
    add_received(2, second)
    for copy in copies[: -len(summing)]:
        copy.wait_send()
    total, rest = end_sum(1, summing)
    rest = rest + pltpu.roll(total, 64, 1)

    def scalar(k):
        return total[:, k : k + 1], rest[:, k : k + 1]

    norm0, energy0, square, bend = (scalar(k) for k in range(4))
    alpha0 = norm0[0] / energy0[0]
    lack = product_less(alpha0, energy0, norm0)
    excess = product_less(alpha0, square, energy0)
    curve = product_less(alpha0, bend, square)
    norm1 = alpha0 * excess - lack
    beta = norm1 / norm0[0]
    energy1 = (alpha0 * curve - excess) + beta * (beta * energy0[0] - 2.0 * excess)
    alpha1 = norm1 / energy1

    res0 = resid[...]
    image0 = image[...]
    res1 = res0 - alpha0 * image0
    image1 = (image0 - alpha0 * second[...]) + beta * image0
    solved = (SCALE * alpha0) * res0 + (SCALE * alpha1) * (res1 + beta * res0)
    left = res1 - alpha1 * image1
    sol_ref[...] = solved[0:ROWS]
    res_ref[...] = left[0:ROWS]
    for copy in summing:
        copy.wait_send()


def solution(mesh):
    n_px = mesh.shape["px"]
    n_py = mesh.shape["py"]
    count = 3 * 8 + (n_px - 1 + n_py - 1)
    coef, ahead, back = tables()

    def body(right_side, geometry, shift, node_order, elem_counts, share_lists):
        vmem = pl.BlockSpec(memory_space=pltpu.VMEM)
        hbm = pl.BlockSpec(memory_space=pltpu.HBM)
        plane = jax.ShapeDtypeStruct((ROWS, LANES), jnp.float32)

        def stay(x):
            return pltpu.with_memory_space_constraint(x, pltpu.HBM)

        vector = pltpu.VMEM((PAD, LANES), jnp.float32)
        solved, left = pl.pallas_call(
            functools.partial(kernel, n_px, n_py),
            out_shape=(plane, plane),
            in_specs=[hbm] * 4 + [vmem] + [hbm] * 4,
            out_specs=(vmem, vmem),
            scratch_shapes=[
                pltpu.VMEM((1, ROWS * LANES), jnp.float32),
                pltpu.VMEM((3, ELEMS, 4 * LANES), jnp.float32),
                pltpu.VMEM((1, ELEMS), jnp.float32),
                pltpu.VMEM((ELEMS, 4 * LANES), jnp.int32),
                pltpu.VMEM((4, FACE + 2 * DIAG), jnp.int32),
                pltpu.VMEM(coef.shape, jnp.float32),
                pltpu.VMEM(ahead.shape, jnp.float32),
                pltpu.VMEM(back.shape, jnp.float32),
                pltpu.VMEM((ELEMS, LANES), jnp.float32),
                vector,
                vector,
                vector,
                vector,
                pltpu.VMEM((8 * ELEMS + 8, LANES), jnp.float32),
                pltpu.VMEM((8 * ELEMS + 8, LANES), jnp.float32),
                pltpu.VMEM((3, PAD, LANES), jnp.float32),
                pltpu.VMEM((8 * ELEMS + 8, LANES), jnp.int32),
                pltpu.VMEM((80, LANES), jnp.int32),
                pltpu.VMEM((8, LANES), jnp.int32),
                pltpu.VMEM((8, LANES), jnp.int32),
                vector,
                pltpu.VMEM((8, LANES), jnp.float32),
                pltpu.VMEM((8 * FACE_ROWS, LANES), jnp.float32),
                pltpu.VMEM((4 * FACE_ROWS + 8, LANES), jnp.int32),
                pltpu.VMEM((4 * FACE_ROWS, LANES), jnp.int32),
                pltpu.VMEM((8, 4 * LANES), jnp.int32),
                pltpu.VMEM((3 * TURN, LANES), jnp.float32),
                pltpu.VMEM((3 * TURN, LANES), jnp.float32),
                pltpu.VMEM((3 * 32, LANES), jnp.float32),
                pltpu.VMEM((n_px + n_py, 1, LANES), jnp.float32),
                pltpu.SemaphoreType.DMA((count,)),
                pltpu.SemaphoreType.DMA((count,)),
                pltpu.SemaphoreType.DMA((8,)),
            ],
            compiler_params=pltpu.CompilerParams(
                collective_id=0, has_side_effects=True, vmem_limit_bytes=32 * 2**20
            ),
            cost_estimate=pl.CostEstimate(
                flops=10**8, bytes_accessed=2 * 10**6, transcendentals=0
            ),
        )(
            stay(right_side[0]),
            stay(geometry[0, 0]),
            stay(shift[0]),
            stay(node_order[0, 0]),
            elem_counts,
            stay(share_lists[0, 0]),
            stay(jnp.asarray(coef)),
            stay(jnp.asarray(ahead)),
            stay(jnp.asarray(back)),
        )
        shape = (1, 1, ROWS * LANES)
        return solved.reshape(shape), left.reshape(shape)

    return jax.shard_map(
        body,
        mesh=mesh,
        in_specs=(
            P("px", "py", None),
            P("px", "py", None, None, None),
            P("px", "py", None),
            P("px", "py", None, None),
            P("px", "py"),
            P("px", "py", None, None),
        ),
        out_specs=(P("px", "py", None), P("px", "py", None)),
        check_vma=False,
    )
```

```python
import functools

import jax
import jax.numpy as jnp
import numpy as np
from jax import lax
from jax.experimental import pallas as pl
from jax.experimental.pallas import tpu as pltpu
from jax.sharding import PartitionSpec as P

STRIDE = 344
FACE = 1280
DIAG = 128
ELEMS = 48
LANES = 128
ROWS = 129
PAD = 136
FACE_ROWS = FACE // LANES
TURN = 80
SCALE = 2.0**-16
ROW_OF = [e * STRIDE // LANES for e in range(ELEMS)]
LOWER = (1, 3, 2, 3)
UPPER = (0, 2, 0, 1)
FACE_STEPS = ((1, 0), (-1, 0), (0, 1), (0, -1))
DIAG_STEPS = ((1, 1), (1, -1), (-1, 1), (-1, -1))
DIAG_LIST = (0, 0, 1, 1)


def gll_derivative():
    degree = 7
    points = np.array(
        [
            -1.0,
            -0.8717401485096066,
            -0.5917001814331423,
            -0.2092992179024789,
            0.2092992179024789,
            0.5917001814331423,
            0.8717401485096066,
            1.0,
        ]
    )
    before = np.ones(8)
    current = points * 1.0
    for order in range(1, degree):
        following = ((2 * order + 1) * points * current - order * before) / (order + 1)
        before = current
        current = following
    same = np.arange(8)[:, None] == np.arange(8)[None, :]
    spacing = np.where(same, 1.0, points[:, None] - points[None, :])
    matrix = np.where(same, 0.0, current[:, None] / (current[None, :] * spacing))
    corner = np.array([-14.0, 0.0, 0.0, 0.0, 0.0, 0.0, 0.0, 14.0])
    return matrix + np.where(same, corner[:, None], 0.0)


def tables():
    deriv = gll_derivative()
    half = np.arange(LANES) // 64

    def lanes_of(matrix):
        rows = []
        for out in range(4):
            for src in range(4):
                rows.append(matrix[2 * out + half, 2 * src + half])
                rows.append(matrix[2 * out + half, 2 * src + 1 - half])
        return np.stack(rows)

    coef = np.concatenate([lanes_of(deriv), SCALE * lanes_of(deriv.T)])
    second = np.kron(np.eye(2), np.kron(deriv, np.eye(8)))
    third = np.kron(np.eye(16), deriv)
    ahead = np.concatenate([second.T, third.T], axis=1)
    back = SCALE * np.concatenate([second, third], axis=0)
    return tuple(np.asarray(t, np.float32) for t in (coef, ahead, back))


def take_lanes(values, lanes):
    return jnp.take_along_axis(values, lanes, axis=1, mode="promise_in_bounds")


def pick(sources, index):
    high = index >> 7
    lanes = index & 127
    total = None
    for j, source in enumerate(sources):
        found = take_lanes(source, lanes)
        total = jnp.where(high == j, found, 0.0 if total is None else total)
    return total


def sum_exactly(rows):
    errors = []
    while len(rows) > 1:
        sums_of = []
        for x, y in zip(rows[::2], rows[1::2]):
            total = x + y
            part = total - x
            errors.append((x - (total - part)) + (y - part))
            sums_of.append(total)
        rows = sums_of
    while len(errors) > 1:
        odd = errors[len(errors) // 2 * 2 :]
        errors = [x + y for x, y in zip(errors[::2], errors[1::2])] + odd
    return rows[0], errors[0]


def split(x):
    small = x * 2.0**-16
    wide = small * 4097.0
    high = (wide - (wide - small)) * 2.0**16
    return high, x - high


def product_less(factor, times, less):
    product = factor * times[0]
    (f_high, f_low), (t_high, t_low) = split(factor), split(times[0])
    error = ((f_high * t_high - product) + f_high * t_low + f_low * t_high) + f_low * t_low
    return (product - less[0]) + ((error - less[1]) + factor * times[1])


def eight(row):
    return jnp.broadcast_to(row, (8, row.shape[1]))


def iota(shape, dim):
    return lax.broadcasted_iota(jnp.int32, shape, dim)


def as_bf16(values):
    return values.astype(jnp.float32).astype(jnp.bfloat16)


def one_hot_lanes(low, row_number):
    low = as_bf16(low)
    one = jnp.ones((LANES, LANES), jnp.bfloat16)
    zero = jnp.zeros((LANES, LANES), jnp.bfloat16)
    return jnp.concatenate(
        [
            jnp.where(row_number == low[:, at : at + LANES], one, zero)
            for at in range(0, low.shape[1], LANES)
        ],
        axis=1,
    )


def over_lanes(left, right):
    return lax.dot_general(
        left, right, (((1,), (1,)), ((), ())), preferred_element_type=jnp.float32
    )


def inverse_rows(high, low, groups, row_number):
    count = high.shape[1]
    number = iota((groups, count), 1) + 1
    hit = high == iota((groups, count), 0)
    tens = jnp.where(hit, number >> 4, 0).astype(jnp.float32)
    ones = jnp.where(hit, number & 15, 0).astype(jnp.float32)
    left = jnp.concatenate([tens, ones], axis=0).astype(jnp.bfloat16)
    found = over_lanes(left, one_hot_lanes(low, row_number))
    return (16.0 * found[:groups] + found[groups:]).astype(jnp.int32) - 1


def kernel(
    n_px,
    n_py,
    rhs_hbm,
    geo_hbm,
    shift_hbm,
    order_hbm,
    count_ref,
    lists_hbm,
    coef_hbm,
    ahead_hbm,
    back_hbm,
    sol_ref,
    res_ref,
    rhs_ref,
    geo_ref,
    shift_ref,
    order_ref,
    lists_ref,
    coef_ref,
    ahead_ref,
    back_ref,
    factors,
    resid,
    image,
    second,
    part,
    windows,
    spread,
    sums,
    elem_inv,
    face_inv,
    cross_inv,
    wrap_inv,
    inv_mult,
    cross_src,
    stack,
    list_idx,
    inv_idx,
    wrap_idx,
    send,
    recv,
    recv_diag,
    red,
    send_sem,
    recv_sem,
    load_sem,
):
    loads = {}
    for number, (name, src, dst) in enumerate(
        (
            ("lists", lists_hbm, lists_ref),
            ("rhs", rhs_hbm, rhs_ref),
            ("order", order_hbm, order_ref),
            ("shift", shift_hbm, shift_ref),
            ("ahead", ahead_hbm, ahead_ref),
            ("geo", geo_hbm, geo_ref),
            ("back", back_hbm, back_ref),
            ("coef", coef_hbm, coef_ref),
        )
    ):
        loads[name] = pltpu.make_async_copy(src, dst, load_sem.at[number])
        loads[name].start()

    px = lax.axis_index("px")
    py = lax.axis_index("py")

    def moved(step_x, step_y):
        return (lax.rem(px + step_x + n_px, n_px), lax.rem(py + step_y + n_py, n_py))

    sizes = (n_px, n_py)

    def place(stage):
        return px if stage == 0 else py

    def far_first(size):
        return sorted(range(1, size), key=lambda d: (-min(d, size - d), d))

    def partners(stage):
        if stage == 0:
            return [(lax.rem(px + d, n_px), py) for d in far_first(n_px)]
        return [(px, lax.rem(py + d, n_py)) for d in far_first(n_py)]

    everyone = [moved(*step) for step in FACE_STEPS + DIAG_STEPS]
    everyone += partners(0) + partners(1)
    barrier = pltpu.get_barrier_semaphore()
    for other in everyone:
        pl.semaphore_signal(
            barrier, inc=1, device_id=other, device_id_type=pl.DeviceIdType.MESH
        )

    copies = []

    def start_copy(src, dst, other):
        number = len(copies)
        copy = pltpu.make_async_remote_copy(
            src_ref=src,
            dst_ref=dst,
            send_sem=send_sem.at[number],
            recv_sem=recv_sem.at[number],
            device_id=other,
            device_id_type=pl.DeviceIdType.MESH,
        )
        copy.start()
        copies.append(copy)
        return copy

    def start_exchange(turn):
        started = []
        for f, step in enumerate(FACE_STEPS):
            started.append(
                start_copy(
                    send.at[pl.ds(TURN * turn + 16 * f, 16)],
                    recv.at[pl.ds(TURN * turn + 16 * (f ^ 1), 16)],
                    moved(*step),
                )
            )
        for d, step in enumerate(DIAG_STEPS):
            started.append(
                start_copy(
                    send.at[pl.ds(TURN * turn + 16 * DIAG_LIST[d] + 8, 8)],
                    recv_diag.at[pl.ds(32 * turn + 8 * (3 - d), 8)],
                    moved(*step),
                )
            )
        return started

    def start_sum(stage, row):
        mine = stage * n_px + place(stage)
        red[pl.ds(mine, 1)] = row[None]
        return [start_copy(red.at[mine], red.at[mine], other) for other in partners(stage)]

    def end_sum(stage, started):
        for copy in started:
            copy.wait_recv()
        return sum_exactly([red[stage * n_px + slot] for slot in range(sizes[stage])])

    live = count_ref[...]

    half = FACE_ROWS // 2

    def pair_up(target, at, upper, lower):
        target[at : at + 4, :] = upper
        target[at + 4 : at + 8, :] = lower

    def stack_rows(source, first, step):
        for j in range(FACE_ROWS):
            rows = source[pl.ds(first + j, 4, stride=step), :]
            pair_up(stack, 8 * j, rows, rows)
        return [stack[8 * j : 8 * j + 8, :] for j in range(FACE_ROWS)]

    def fill_send(turn, source):
        rows = stack_rows(source, 0, FACE_ROWS)
        for i in range(half):
            found = pick(rows, list_idx[8 * i : 8 * i + 8, :])
            send[pl.ds(TURN * turn + i, 4, stride=16), :] = found[0:4]
            send[pl.ds(TURN * turn + i + half, 4, stride=16), :] = found[4:8]
        first = 4 * FACE_ROWS
        for at, q in enumerate(LOWER + UPPER):
            cross_src[at : at + 1, :] = source[first + q : first + q + 1, :]
        found = pick([cross_src[...]], list_idx[8 * half : 8 * half + 8, :])
        send[pl.ds(TURN * turn + FACE_ROWS, 4, stride=16), :] = found[0:4]
        send[pl.ds(TURN * turn + FACE_ROWS + 1, 4, stride=16), :] = found[4:8]

    def add_received(turn, target):
        rows = stack_rows(recv, TURN * turn, 16)
        for i in range(half):
            found = pick(rows, inv_idx[8 * i : 8 * i + 8, :])
            target[pl.ds(i, 4, stride=FACE_ROWS), :] += found[0:4]
            target[pl.ds(i + half, 4, stride=FACE_ROWS), :] += found[4:8]
        for part in range(2):
            at = TURN * turn + FACE_ROWS + part
            cross_src[4 * part : 4 * part + 4, :] = recv[pl.ds(at, 4, stride=16), :]
        for row, q, i in ((2, 2, 2), (3, 3, 3), (6, 0, 2), (7, 1, 3)):
            at = 32 * turn + 8 * q + i
            cross_src[row : row + 1, :] += recv_diag[at : at + 1, :]
        found = pick([cross_src[...]], cross_inv[...])
        first = 4 * FACE_ROWS
        for at, q in enumerate(LOWER + UPPER):
            target[first + q : first + q + 1, :] += found[at : at + 1]

    element = iota((ELEMS, LANES), 0)
    offset = (element * STRIDE) & 127
    is_last = element == live - 1

    def orders(c):
        return order_ref[:, c * LANES : (c + 1) * LANES]

    def last_row(values):
        return jnp.sum(jnp.where(is_last, values, jnp.zeros_like(values)), axis=0, keepdims=True)

    def set_up():
        row_number = as_bf16(iota((LANES, LANES), 0))
        for f in range(4):
            row = lists_ref[f : f + 1, 0:FACE]
            face_inv[16 * f : 16 * f + 16, :] = inverse_rows(row >> 7, row & 127, 16, row_number)
            for part in range(2):
                at = FACE + part * DIAG
                row = lists_ref[f : f + 1, at : at + DIAG]
                number = (iota((8, DIAG), 1) + 1).astype(jnp.float32).astype(jnp.bfloat16)
                found = over_lanes(number, one_hot_lanes(row, row_number))
                cross_inv[4 * part + f : 4 * part + f + 1, :] = found[0:1].astype(jnp.int32) - 1
        for i in range(half):
            pair_up(
                inv_idx,
                8 * i,
                face_inv[pl.ds(i, 4, stride=16), :],
                face_inv[pl.ds(i + half, 4, stride=16), :],
            )
        inv_mult[...] = jnp.ones_like(inv_mult)
        for f in range(4):
            named = face_inv[16 * f : 16 * f + FACE_ROWS, :] >= 0
            inv_mult[f * FACE_ROWS : (f + 1) * FACE_ROWS, :] = jnp.where(named, 0.5, 1.0)
        for q in range(4):
            copies_of = jnp.ones((1, LANES), jnp.float32)
            for part, regions in enumerate((LOWER, UPPER)):
                for f, region in enumerate(regions):
                    if region == q:
                        row = cross_inv[4 * part + f : 4 * part + f + 1, :]
                        copies_of = copies_of + jnp.where(row >= 0, 1.5, 0.0)
            at = 4 * FACE_ROWS + q
            inv_mult[at : at + 1, :] = 1.0 / copies_of

        @pl.loop(0, ELEMS // 16)
        def _(group):
            block = order_ref[pl.ds(pl.multiple_of(16 * group, 16), 16), :]
            for s in range(16):
                e = 16 * group + s
                row = block[s : s + 1]
                shifted = row + s * STRIDE % LANES
                own = jnp.where(live <= e, 0, jnp.where(live == e + 1, STRIDE, 4 * LANES))
                high = jnp.where(row >= own, 7, shifted >> 7)
                elem_inv[pl.ds(pl.multiple_of(8 * e, 8), 8), :] = inverse_rows(
                    high, shifted & 127, 8, row_number
                )

        wrapped = jnp.concatenate([last_row(orders(c)) for c in range(4)], axis=1) - STRIDE
        wrap_inv[...] = inverse_rows(wrapped >> 7, wrapped & 127, 8, row_number)
        wrap_idx[...] = eight(wrapped)

    def derivative(chunks, first):
        swapped = [pltpu.roll(u, 64, 1) for u in chunks]
        result = []
        for out in range(4):
            total = None
            for src in range(4):
                at = first + (out * 4 + src) * 2
                term = coef_ref[at : at + 1, :] * chunks[src]
                total = term if total is None else total + term
                total = total + coef_ref[at + 1 : at + 2, :] * swapped[src]
            result.append(total)
        return result

    def stacked(k):
        return jnp.concatenate(
            [geo_ref[k, :, c * LANES : (c + 1) * LANES] for c in range(4)], axis=0
        )

    def operate(source):
        for e, row in enumerate(ROW_OF):
            windows[8 * e : 8 * e + 8, :] = source[row : row + 8, :]
        rows = [windows[pl.ds(k, ELEMS, stride=8), :] for k in range(5)]
        chunks = []
        for c in range(4):
            order = orders(c)
            around = pick(
                [eight(source[0:1, :]), eight(source[1:2, :])],
                wrap_idx[:, c * LANES : (c + 1) * LANES],
            )[0:1]
            values = pick(rows, order + offset)
            chunks.append(jnp.where(is_last & (order >= STRIDE), around, values))
        exact = lax.Precision.HIGHEST
        narrow = jnp.concatenate(chunks, axis=0)
        grads = jnp.dot(
            narrow, ahead_ref[...], precision=exact, preferred_element_type=jnp.float32
        )
        fluxes = jnp.concatenate(
            [stacked(1) * grads[:, :LANES], stacked(2) * grads[:, LANES:]], axis=1
        )
        terms = jnp.dot(
            fluxes, back_ref[...], precision=exact, preferred_element_type=jnp.float32
        )
        grad = derivative(chunks, 0)
        grad = [geo_ref[0, :, c * LANES : (c + 1) * LANES] * grad[c] for c in range(4)]
        first = derivative(grad, 32)
        factor = factors[...]
        result = [
            terms[c * ELEMS : (c + 1) * ELEMS] + first[c] + factor * chunks[c] for c in range(4)
        ]
        for k in range(5):
            spread[pl.ds(k, ELEMS, stride=8), :] = pick(
                result, elem_inv[pl.ds(k, ELEMS, stride=8), :]
            )
        for e, row in enumerate(ROW_OF):
            sums[e % 3, row : row + 8, :] = spread[8 * e : 8 * e + 8, :]
        sums[0, 0:8, :] += pick([eight(last_row(r)) for r in result], wrap_inv[...])
        return sums[0] + sums[1] + sums[2]

    lane = iota((1, LANES), 1)

    def dots(first, row, *products):
        for k, product in enumerate(products, first):
            total = jnp.sum(jnp.sum(product, axis=0, keepdims=True), axis=1, keepdims=True)
            row = jnp.where(lane == k, total, row)
        return row

    send[...] = jnp.zeros_like(send)
    spread[...] = jnp.zeros_like(spread)
    sums[...] = jnp.zeros_like(sums)
    resid[...] = jnp.zeros_like(resid)
    loads["lists"].wait()
    loads["rhs"].wait()
    for i in range(half):
        pair_up(
            list_idx,
            8 * i,
            lists_ref[:, i * LANES : (i + 1) * LANES],
            lists_ref[:, (i + half) * LANES : (i + half + 1) * LANES],
        )
    pair_up(
        list_idx,
        8 * half,
        lists_ref[:, FACE : FACE + DIAG],
        lists_ref[:, FACE + DIAG : FACE + 2 * DIAG],
    )
    for i in range(ROWS):
        resid[i : i + 1, :] = rhs_ref[:, i * LANES : (i + 1) * LANES]
    slot = iota((ROWS, LANES), 0) * LANES + iota((ROWS, LANES), 1)
    resid[0:ROWS, :] = jnp.where(slot < live * STRIDE, resid[0:ROWS, :], 0.0)
    fill_send(0, resid)
    pl.semaphore_wait(barrier, len(everyone))
    exchange = start_exchange(0)
    loads["order"].wait()
    loads["shift"].wait()
    set_up()
    same = iota((ELEMS, ELEMS), 0) == iota((ELEMS, ELEMS), 1)
    column = jnp.sum(jnp.where(same, shift_ref[...], 0.0), axis=1, keepdims=True)
    factors[...] = jnp.broadcast_to(SCALE * column, (ELEMS, LANES))
    for name in ("ahead", "geo", "back", "coef"):
        loads[name].wait()
    for copy in exchange:
        copy.wait_recv()
    add_received(0, resid)

    part[...] = operate(resid)
    image[...] = part[...]
    fill_send(1, image)
    exchange = start_exchange(1)
    res0 = resid[...]
    row = jnp.zeros((1, LANES), jnp.float32)
    row = dots(0, row, res0 * res0 * inv_mult[...], res0 * part[...])
    for copy in exchange:
        copy.wait_recv()
    add_received(1, image)

    part[...] = operate(image)
    image0 = image[...]
    row = dots(2, row, image0 * image0 * inv_mult[...], image0 * part[...])
    summing = start_sum(0, row)
    second[...] = part[...]
    fill_send(2, second)
    exchange = start_exchange(2)
    total, rest = end_sum(0, summing)
    summing = start_sum(1, jnp.where(lane < 64, total, pltpu.roll(rest, 64, 1)))
    for copy in exchange:
        copy.wait_recv()
    add_received(2, second)
    for copy in copies[: -len(summing)]:
        copy.wait_send()
    total, rest = end_sum(1, summing)
    rest = rest + pltpu.roll(total, 64, 1)

    def scalar(k):
        return total[:, k : k + 1], rest[:, k : k + 1]

    norm0, energy0, square, bend = (scalar(k) for k in range(4))
    alpha0 = norm0[0] / energy0[0]
    lack = product_less(alpha0, energy0, norm0)
    excess = product_less(alpha0, square, energy0)
    curve = product_less(alpha0, bend, square)
    norm1 = alpha0 * excess - lack
    beta = norm1 / norm0[0]
    energy1 = (alpha0 * curve - excess) + beta * (beta * energy0[0] - 2.0 * excess)
    alpha1 = norm1 / energy1

    res0 = resid[...]
    image0 = image[...]
    res1 = res0 - alpha0 * image0
    image1 = (image0 - alpha0 * second[...]) + beta * image0
    solved = (SCALE * alpha0) * res0 + (SCALE * alpha1) * (res1 + beta * res0)
    left = res1 - alpha1 * image1
    sol_ref[...] = solved[0:ROWS]
    res_ref[...] = left[0:ROWS]
    for copy in summing:
        copy.wait_send()


def solution(mesh):
    n_px = mesh.shape["px"]
    n_py = mesh.shape["py"]
    count = 3 * 8 + (n_px - 1 + n_py - 1)
    coef, ahead, back = tables()

    def body(right_side, geometry, shift, node_order, elem_counts, share_lists):
        vmem = pl.BlockSpec(memory_space=pltpu.VMEM)
        hbm = pl.BlockSpec(memory_space=pltpu.HBM)
        plane = jax.ShapeDtypeStruct((ROWS, LANES), jnp.float32)

        def stay(x):
            return pltpu.with_memory_space_constraint(x, pltpu.HBM)

        vector = pltpu.VMEM((PAD, LANES), jnp.float32)
        solved, left = pl.pallas_call(
            functools.partial(kernel, n_px, n_py),
            out_shape=(plane, plane),
            in_specs=[hbm] * 4 + [vmem] + [hbm] * 4,
            out_specs=(vmem, vmem),
            scratch_shapes=[
                pltpu.VMEM((1, ROWS * LANES), jnp.float32),
                pltpu.VMEM((3, ELEMS, 4 * LANES), jnp.float32),
                pltpu.VMEM((1, ELEMS), jnp.float32),
                pltpu.VMEM((ELEMS, 4 * LANES), jnp.int32),
                pltpu.VMEM((4, FACE + 2 * DIAG), jnp.int32),
                pltpu.VMEM(coef.shape, jnp.float32),
                pltpu.VMEM(ahead.shape, jnp.float32),
                pltpu.VMEM(back.shape, jnp.float32),
                pltpu.VMEM((ELEMS, LANES), jnp.float32),
                vector,
                vector,
                vector,
                vector,
                pltpu.VMEM((8 * ELEMS + 8, LANES), jnp.float32),
                pltpu.VMEM((8 * ELEMS + 8, LANES), jnp.float32),
                pltpu.VMEM((3, PAD, LANES), jnp.float32),
                pltpu.VMEM((8 * ELEMS + 8, LANES), jnp.int32),
                pltpu.VMEM((80, LANES), jnp.int32),
                pltpu.VMEM((8, LANES), jnp.int32),
                pltpu.VMEM((8, LANES), jnp.int32),
                vector,
                pltpu.VMEM((8, LANES), jnp.float32),
                pltpu.VMEM((8 * FACE_ROWS, LANES), jnp.float32),
                pltpu.VMEM((4 * FACE_ROWS + 8, LANES), jnp.int32),
                pltpu.VMEM((4 * FACE_ROWS, LANES), jnp.int32),
                pltpu.VMEM((8, 4 * LANES), jnp.int32),
                pltpu.VMEM((3 * TURN, LANES), jnp.float32),
                pltpu.VMEM((3 * TURN, LANES), jnp.float32),
                pltpu.VMEM((3 * 32, LANES), jnp.float32),
                pltpu.VMEM((n_px + n_py, 1, LANES), jnp.float32),
                pltpu.SemaphoreType.DMA((count,)),
                pltpu.SemaphoreType.DMA((count,)),
                pltpu.SemaphoreType.DMA((8,)),
            ],
            compiler_params=pltpu.CompilerParams(
                collective_id=0, has_side_effects=True, vmem_limit_bytes=32 * 2**20
            ),
            cost_estimate=pl.CostEstimate(
                flops=10**8, bytes_accessed=2 * 10**6, transcendentals=0
            ),
        )(
            stay(right_side[0]),
            stay(geometry[0, 0]),
            stay(shift[0]),
            stay(node_order[0, 0]),
            elem_counts,
            stay(share_lists[0, 0]),
            stay(jnp.asarray(coef)),
            stay(jnp.asarray(ahead)),
            stay(jnp.asarray(back)),
        )
        shape = (1, 1, ROWS * LANES)
        return solved.reshape(shape), left.reshape(shape)

    return jax.shard_map(
        body,
        mesh=mesh,
        in_specs=(
            P("px", "py", None),
            P("px", "py", None, None, None),
            P("px", "py", None),
            P("px", "py", None, None),
            P("px", "py"),
            P("px", "py", None, None),
        ),
        out_specs=(P("px", "py", None), P("px", "py", None)),
        check_vma=False,
    )
```

```python
import functools

import jax
import jax.numpy as jnp
import numpy as np
from jax import lax
from jax.experimental import pallas as pl
from jax.experimental.pallas import tpu as pltpu
from jax.sharding import PartitionSpec as P

STRIDE = 344
FACE = 1280
DIAG = 128
ELEMS = 48
LANES = 128
ROWS = 129
PAD = 136
FACE_ROWS = FACE // LANES
TURN = 80
SCALE = 2.0**-16
ROW_OF = [e * STRIDE // LANES for e in range(ELEMS)]
LOWER = (1, 3, 2, 3)
UPPER = (0, 2, 0, 1)
FACE_STEPS = ((1, 0), (-1, 0), (0, 1), (0, -1))
DIAG_STEPS = ((1, 1), (1, -1), (-1, 1), (-1, -1))
DIAG_LIST = (0, 0, 1, 1)


def gll_derivative():
    degree = 7
    points = np.array(
        [
            -1.0,
            -0.8717401485096066,
            -0.5917001814331423,
            -0.2092992179024789,
            0.2092992179024789,
            0.5917001814331423,
            0.8717401485096066,
            1.0,
        ]
    )
    before = np.ones(8)
    current = points * 1.0
    for order in range(1, degree):
        following = ((2 * order + 1) * points * current - order * before) / (order + 1)
        before = current
        current = following
    same = np.arange(8)[:, None] == np.arange(8)[None, :]
    spacing = np.where(same, 1.0, points[:, None] - points[None, :])
    matrix = np.where(same, 0.0, current[:, None] / (current[None, :] * spacing))
    corner = np.array([-14.0, 0.0, 0.0, 0.0, 0.0, 0.0, 0.0, 14.0])
    return matrix + np.where(same, corner[:, None], 0.0)


def tables():
    deriv = gll_derivative()
    half = np.arange(LANES) // 64

    def lanes_of(matrix):
        rows = []
        for out in range(4):
            for src in range(4):
                rows.append(matrix[2 * out + half, 2 * src + half])
                rows.append(matrix[2 * out + half, 2 * src + 1 - half])
        return np.stack(rows)

    coef = np.concatenate([lanes_of(deriv), SCALE * lanes_of(deriv.T)])
    second = np.kron(np.eye(2), np.kron(deriv, np.eye(8)))
    third = np.kron(np.eye(16), deriv)
    ahead = np.concatenate([second.T, third.T], axis=1)
    back = SCALE * np.concatenate([second, third], axis=0)
    halves = [ahead[:, :LANES], ahead[:, LANES:], back]
    parts = np.concatenate([part for half in halves for part in three_parts(half)], axis=0)
    return np.asarray(coef, np.float32), parts


def three_parts(table):
    rest = np.asarray(table, np.float32)
    parts = []
    for _ in range(3):
        part = rest.astype(jnp.bfloat16)
        parts.append(part)
        rest = rest - part.astype(np.float32)
    return parts


def three_ways(values):
    first = values.astype(jnp.bfloat16)
    rest = values - first.astype(jnp.float32)
    second = rest.astype(jnp.bfloat16)
    return first, second, (rest - second.astype(jnp.float32)).astype(jnp.bfloat16)


def product(pieces, table):
    left = jnp.concatenate(pieces, axis=1)
    return jnp.dot(left, table, preferred_element_type=jnp.float32)


def take_lanes(values, lanes):
    return jnp.take_along_axis(values, lanes, axis=1, mode="promise_in_bounds")


def pick(sources, index):
    high = index >> 7
    lanes = index & 127
    total = None
    for j, source in enumerate(sources):
        found = take_lanes(source, lanes)
        total = jnp.where(high == j, found, 0.0 if total is None else total)
    return total


def sum_exactly(rows):
    errors = []
    while len(rows) > 1:
        sums_of = []
        for x, y in zip(rows[::2], rows[1::2]):
            total = x + y
            part = total - x
            errors.append((x - (total - part)) + (y - part))
            sums_of.append(total)
        rows = sums_of
    while len(errors) > 1:
        odd = errors[len(errors) // 2 * 2 :]
        errors = [x + y for x, y in zip(errors[::2], errors[1::2])] + odd
    return rows[0], errors[0]


def split(x):
    small = x * 2.0**-16
    wide = small * 4097.0
    high = (wide - (wide - small)) * 2.0**16
    return high, x - high


def product_less(factor, times, less):
    product = factor * times[0]
    (f_high, f_low), (t_high, t_low) = split(factor), split(times[0])
    error = ((f_high * t_high - product) + f_high * t_low + f_low * t_high) + f_low * t_low
    return (product - less[0]) + ((error - less[1]) + factor * times[1])


def eight(row):
    return jnp.broadcast_to(row, (8, row.shape[1]))


def iota(shape, dim):
    return lax.broadcasted_iota(jnp.int32, shape, dim)


def as_bf16(values):
    return values.astype(jnp.float32).astype(jnp.bfloat16)


def one_hot_lanes(low, row_number):
    low = as_bf16(low)
    one = jnp.ones((LANES, LANES), jnp.bfloat16)
    zero = jnp.zeros((LANES, LANES), jnp.bfloat16)
    return jnp.concatenate(
        [
            jnp.where(row_number == low[:, at : at + LANES], one, zero)
            for at in range(0, low.shape[1], LANES)
        ],
        axis=1,
    )


def over_lanes(left, right):
    return lax.dot_general(
        left, right, (((1,), (1,)), ((), ())), preferred_element_type=jnp.float32
    )


def inverse_rows(high, low, groups, row_number):
    count = high.shape[1]
    number = iota((groups, count), 1) + 1
    hit = high == iota((groups, count), 0)
    tens = jnp.where(hit, number >> 4, 0).astype(jnp.float32)
    ones = jnp.where(hit, number & 15, 0).astype(jnp.float32)
    left = jnp.concatenate([tens, ones], axis=0).astype(jnp.bfloat16)
    found = over_lanes(left, one_hot_lanes(low, row_number))
    return (16.0 * found[:groups] + found[groups:]).astype(jnp.int32) - 1


def kernel(
    n_px,
    n_py,
    rhs_hbm,
    geo_hbm,
    shift_hbm,
    order_hbm,
    count_ref,
    lists_hbm,
    coef_hbm,
    parts_hbm,
    sol_ref,
    res_ref,
    rhs_ref,
    geo_ref,
    shift_ref,
    order_ref,
    lists_ref,
    coef_ref,
    parts_ref,
    factors,
    resid,
    image,
    second,
    part,
    windows,
    spread,
    sums,
    elem_inv,
    face_inv,
    cross_inv,
    wrap_inv,
    inv_mult,
    cross_src,
    stack,
    list_idx,
    inv_idx,
    wrap_idx,
    send,
    recv,
    recv_diag,
    red,
    send_sem,
    recv_sem,
    load_sem,
):
    loads = {}
    for number, (name, src, dst) in enumerate(
        (
            ("lists", lists_hbm, lists_ref),
            ("rhs", rhs_hbm, rhs_ref),
            ("order", order_hbm, order_ref),
            ("shift", shift_hbm, shift_ref),
            ("parts", parts_hbm, parts_ref),
            ("geo", geo_hbm, geo_ref),
            ("coef", coef_hbm, coef_ref),
        )
    ):
        loads[name] = pltpu.make_async_copy(src, dst, load_sem.at[number])
        loads[name].start()

    px = lax.axis_index("px")
    py = lax.axis_index("py")

    def moved(step_x, step_y):
        return (lax.rem(px + step_x + n_px, n_px), lax.rem(py + step_y + n_py, n_py))

    sizes = (n_px, n_py)

    def place(stage):
        return px if stage == 0 else py

    def far_first(size):
        return sorted(range(1, size), key=lambda d: (-min(d, size - d), d))

    def partners(stage):
        if stage == 0:
            return [(lax.rem(px + d, n_px), py) for d in far_first(n_px)]
        return [(px, lax.rem(py + d, n_py)) for d in far_first(n_py)]

    everyone = [moved(*step) for step in FACE_STEPS + DIAG_STEPS]
    everyone += partners(0) + partners(1)
    barrier = pltpu.get_barrier_semaphore()
    for other in everyone:
        pl.semaphore_signal(
            barrier, inc=1, device_id=other, device_id_type=pl.DeviceIdType.MESH
        )

    copies = []

    def start_copy(src, dst, other):
        number = len(copies)
        copy = pltpu.make_async_remote_copy(
            src_ref=src,
            dst_ref=dst,
            send_sem=send_sem.at[number],
            recv_sem=recv_sem.at[number],
            device_id=other,
            device_id_type=pl.DeviceIdType.MESH,
        )
        copy.start()
        copies.append(copy)
        return copy

    def start_exchange(turn):
        started = []
        for f, step in enumerate(FACE_STEPS):
            started.append(
                start_copy(
                    send.at[pl.ds(TURN * turn + 16 * f, 16)],
                    recv.at[pl.ds(TURN * turn + 16 * (f ^ 1), 16)],
                    moved(*step),
                )
            )
        for d, step in enumerate(DIAG_STEPS):
            started.append(
                start_copy(
                    send.at[pl.ds(TURN * turn + 16 * DIAG_LIST[d] + 8, 8)],
                    recv_diag.at[pl.ds(32 * turn + 8 * (3 - d), 8)],
                    moved(*step),
                )
            )
        return started

    def start_sum(stage, row):
        mine = stage * n_px + place(stage)
        red[pl.ds(mine, 1)] = row[None]
        return [start_copy(red.at[mine], red.at[mine], other) for other in partners(stage)]

    def end_sum(stage, started):
        for copy in started:
            copy.wait_recv()
        return sum_exactly([red[stage * n_px + slot] for slot in range(sizes[stage])])

    live = count_ref[...]

    half = FACE_ROWS // 2

    def pair_up(target, at, upper, lower):
        target[at : at + 4, :] = upper
        target[at + 4 : at + 8, :] = lower

    def stack_rows(source, first, step):
        for j in range(FACE_ROWS):
            rows = source[pl.ds(first + j, 4, stride=step), :]
            pair_up(stack, 8 * j, rows, rows)
        return [stack[8 * j : 8 * j + 8, :] for j in range(FACE_ROWS)]

    def fill_send(turn, source):
        rows = stack_rows(source, 0, FACE_ROWS)
        for i in range(half):
            found = pick(rows, list_idx[8 * i : 8 * i + 8, :])
            send[pl.ds(TURN * turn + i, 4, stride=16), :] = found[0:4]
            send[pl.ds(TURN * turn + i + half, 4, stride=16), :] = found[4:8]
        first = 4 * FACE_ROWS
        for at, q in enumerate(LOWER + UPPER):
            cross_src[at : at + 1, :] = source[first + q : first + q + 1, :]
        found = pick([cross_src[...]], list_idx[8 * half : 8 * half + 8, :])
        send[pl.ds(TURN * turn + FACE_ROWS, 4, stride=16), :] = found[0:4]
        send[pl.ds(TURN * turn + FACE_ROWS + 1, 4, stride=16), :] = found[4:8]

    def add_received(turn, target):
        rows = stack_rows(recv, TURN * turn, 16)
        for i in range(half):
            found = pick(rows, inv_idx[8 * i : 8 * i + 8, :])
            target[pl.ds(i, 4, stride=FACE_ROWS), :] += found[0:4]
            target[pl.ds(i + half, 4, stride=FACE_ROWS), :] += found[4:8]
        for part in range(2):
            at = TURN * turn + FACE_ROWS + part
            cross_src[4 * part : 4 * part + 4, :] = recv[pl.ds(at, 4, stride=16), :]
        for row, q, i in ((2, 2, 2), (3, 3, 3), (6, 0, 2), (7, 1, 3)):
            at = 32 * turn + 8 * q + i
            cross_src[row : row + 1, :] += recv_diag[at : at + 1, :]
        found = pick([cross_src[...]], cross_inv[...])
        first = 4 * FACE_ROWS
        for at, q in enumerate(LOWER + UPPER):
            target[first + q : first + q + 1, :] += found[at : at + 1]

    element = iota((ELEMS, LANES), 0)
    offset = (element * STRIDE) & 127
    is_last = element == live - 1

    def orders(c):
        return order_ref[:, c * LANES : (c + 1) * LANES]

    def last_row(values):
        return jnp.sum(jnp.where(is_last, values, jnp.zeros_like(values)), axis=0, keepdims=True)

    def set_up():
        row_number = as_bf16(iota((LANES, LANES), 0))
        for f in range(4):
            row = lists_ref[f : f + 1, 0:FACE]
            face_inv[16 * f : 16 * f + 16, :] = inverse_rows(row >> 7, row & 127, 16, row_number)
            for part in range(2):
                at = FACE + part * DIAG
                row = lists_ref[f : f + 1, at : at + DIAG]
                number = (iota((8, DIAG), 1) + 1).astype(jnp.float32).astype(jnp.bfloat16)
                found = over_lanes(number, one_hot_lanes(row, row_number))
                cross_inv[4 * part + f : 4 * part + f + 1, :] = found[0:1].astype(jnp.int32) - 1
        for i in range(half):
            pair_up(
                inv_idx,
                8 * i,
                face_inv[pl.ds(i, 4, stride=16), :],
                face_inv[pl.ds(i + half, 4, stride=16), :],
            )
        inv_mult[...] = jnp.ones_like(inv_mult)
        for f in range(4):
            named = face_inv[16 * f : 16 * f + FACE_ROWS, :] >= 0
            inv_mult[f * FACE_ROWS : (f + 1) * FACE_ROWS, :] = jnp.where(named, 0.5, 1.0)
        for q in range(4):
            copies_of = jnp.ones((1, LANES), jnp.float32)
            for part, regions in enumerate((LOWER, UPPER)):
                for f, region in enumerate(regions):
                    if region == q:
                        row = cross_inv[4 * part + f : 4 * part + f + 1, :]
                        copies_of = copies_of + jnp.where(row >= 0, 1.5, 0.0)
            at = 4 * FACE_ROWS + q
            inv_mult[at : at + 1, :] = 1.0 / copies_of

        @pl.loop(0, ELEMS // 16)
        def _(group):
            block = order_ref[pl.ds(pl.multiple_of(16 * group, 16), 16), :]
            for s in range(16):
                e = 16 * group + s
                row = block[s : s + 1]
                shifted = row + s * STRIDE % LANES
                own = jnp.where(live <= e, 0, jnp.where(live == e + 1, STRIDE, 4 * LANES))
                high = jnp.where(row >= own, 7, shifted >> 7)
                elem_inv[pl.ds(pl.multiple_of(8 * e, 8), 8), :] = inverse_rows(
                    high, shifted & 127, 8, row_number
                )

        wrapped = jnp.concatenate([last_row(orders(c)) for c in range(4)], axis=1) - STRIDE
        wrap_inv[...] = inverse_rows(wrapped >> 7, wrapped & 127, 8, row_number)
        wrap_idx[...] = eight(wrapped)

    def derivative(chunks, first):
        swapped = [pltpu.roll(u, 64, 1) for u in chunks]
        result = []
        for out in range(4):
            total = None
            for src in range(4):
                at = first + (out * 4 + src) * 2
                term = coef_ref[at : at + 1, :] * chunks[src]
                total = term if total is None else total + term
                total = total + coef_ref[at + 1 : at + 2, :] * swapped[src]
            result.append(total)
        return result

    def stacked(k):
        return jnp.concatenate(
            [geo_ref[k, :, c * LANES : (c + 1) * LANES] for c in range(4)], axis=0
        )

    def operate(source):
        for e, row in enumerate(ROW_OF):
            windows[8 * e : 8 * e + 8, :] = source[row : row + 8, :]
        rows = [windows[pl.ds(k, ELEMS, stride=8), :] for k in range(5)]
        chunks = []
        for c in range(4):
            order = orders(c)
            around = pick(
                [eight(source[0:1, :]), eight(source[1:2, :])],
                wrap_idx[:, c * LANES : (c + 1) * LANES],
            )[0:1]
            values = pick(rows, order + offset)
            chunks.append(jnp.where(is_last & (order >= STRIDE), around, values))
        a1, a2, a3 = (
            jnp.concatenate(
                [parts_ref[at : at + LANES, :] for at in (k * LANES, (3 + k) * LANES)], axis=1
            )
            for k in range(3)
        )
        ahead = jnp.concatenate([a1, a1, a2, a2, a1, a3], axis=0)
        b1, b2, b3 = (
            parts_ref[(6 + 2 * k) * LANES : (8 + 2 * k) * LANES, :] for k in range(3)
        )
        back_wide = jnp.concatenate([b1, b2], axis=1)
        back_wide = jnp.concatenate([back_wide, back_wide], axis=0)
        back_rest = jnp.concatenate([b1, b3], axis=0)
        u1, u2, u3 = three_ways(jnp.concatenate(chunks, axis=0))
        grads = product([u1, u2, u1, u2, u3, u1], ahead)
        fluxes = jnp.concatenate(
            [stacked(1) * grads[:, :LANES], stacked(2) * grads[:, LANES:]], axis=1
        )
        u1, u2, u3 = three_ways(fluxes)
        wide = product([u1, u2], back_wide)
        terms = product([u3, u1], back_rest) + wide[:, LANES:] + wide[:, :LANES]
        grad = derivative(chunks, 0)
        grad = [geo_ref[0, :, c * LANES : (c + 1) * LANES] * grad[c] for c in range(4)]
        first = derivative(grad, 32)
        factor = factors[...]
        result = [
            terms[c * ELEMS : (c + 1) * ELEMS] + first[c] + factor * chunks[c] for c in range(4)
        ]
        for k in range(5):
            spread[pl.ds(k, ELEMS, stride=8), :] = pick(
                result, elem_inv[pl.ds(k, ELEMS, stride=8), :]
            )
        for e, row in enumerate(ROW_OF):
            sums[e % 3, row : row + 8, :] = spread[8 * e : 8 * e + 8, :]
        sums[0, 0:8, :] += pick([eight(last_row(r)) for r in result], wrap_inv[...])
        return sums[0] + sums[1] + sums[2]

    lane = iota((1, LANES), 1)

    def dots(first, row, *products):
        for k, product in enumerate(products, first):
            total = jnp.sum(jnp.sum(product, axis=0, keepdims=True), axis=1, keepdims=True)
            row = jnp.where(lane == k, total, row)
        return row

    send[...] = jnp.zeros_like(send)
    spread[...] = jnp.zeros_like(spread)
    sums[...] = jnp.zeros_like(sums)
    resid[...] = jnp.zeros_like(resid)
    loads["lists"].wait()
    loads["rhs"].wait()
    for i in range(half):
        pair_up(
            list_idx,
            8 * i,
            lists_ref[:, i * LANES : (i + 1) * LANES],
            lists_ref[:, (i + half) * LANES : (i + half + 1) * LANES],
        )
    pair_up(
        list_idx,
        8 * half,
        lists_ref[:, FACE : FACE + DIAG],
        lists_ref[:, FACE + DIAG : FACE + 2 * DIAG],
    )
    for i in range(ROWS):
        resid[i : i + 1, :] = rhs_ref[:, i * LANES : (i + 1) * LANES]
    slot = iota((ROWS, LANES), 0) * LANES + iota((ROWS, LANES), 1)
    resid[0:ROWS, :] = jnp.where(slot < live * STRIDE, resid[0:ROWS, :], 0.0)
    fill_send(0, resid)
    pl.semaphore_wait(barrier, len(everyone))
    exchange = start_exchange(0)
    loads["order"].wait()
    loads["shift"].wait()
    set_up()
    same = iota((ELEMS, ELEMS), 0) == iota((ELEMS, ELEMS), 1)
    column = jnp.sum(jnp.where(same, shift_ref[...], 0.0), axis=1, keepdims=True)
    factors[...] = jnp.broadcast_to(SCALE * column, (ELEMS, LANES))
    for name in ("parts", "geo", "coef"):
        loads[name].wait()
    for copy in exchange:
        copy.wait_recv()
    add_received(0, resid)

    part[...] = operate(resid)
    image[...] = part[...]
    fill_send(1, image)
    exchange = start_exchange(1)
    res0 = resid[...]
    row = jnp.zeros((1, LANES), jnp.float32)
    row = dots(0, row, res0 * res0 * inv_mult[...], res0 * part[...])
    for copy in exchange:
        copy.wait_recv()
    add_received(1, image)

    part[...] = operate(image)
    image0 = image[...]
    row = dots(2, row, image0 * image0 * inv_mult[...], image0 * part[...])
    summing = start_sum(0, row)
    second[...] = part[...]
    fill_send(2, second)
    exchange = start_exchange(2)
    total, rest = end_sum(0, summing)
    summing = start_sum(1, jnp.where(lane < 64, total, pltpu.roll(rest, 64, 1)))
    for copy in exchange:
        copy.wait_recv()
    add_received(2, second)
    for copy in copies[: -len(summing)]:
        copy.wait_send()
    total, rest = end_sum(1, summing)
    rest = rest + pltpu.roll(total, 64, 1)

    def scalar(k):
        return total[:, k : k + 1], rest[:, k : k + 1]

    norm0, energy0, square, bend = (scalar(k) for k in range(4))
    alpha0 = norm0[0] / energy0[0]
    lack = product_less(alpha0, energy0, norm0)
    excess = product_less(alpha0, square, energy0)
    curve = product_less(alpha0, bend, square)
    norm1 = alpha0 * excess - lack
    beta = norm1 / norm0[0]
    energy1 = (alpha0 * curve - excess) + beta * (beta * energy0[0] - 2.0 * excess)
    alpha1 = norm1 / energy1

    res0 = resid[...]
    image0 = image[...]
    res1 = res0 - alpha0 * image0
    image1 = (image0 - alpha0 * second[...]) + beta * image0
    solved = (SCALE * alpha0) * res0 + (SCALE * alpha1) * (res1 + beta * res0)
    left = res1 - alpha1 * image1
    sol_ref[...] = solved[0:ROWS]
    res_ref[...] = left[0:ROWS]
    for copy in summing:
        copy.wait_send()


def solution(mesh):
    n_px = mesh.shape["px"]
    n_py = mesh.shape["py"]
    count = 3 * 8 + (n_px - 1 + n_py - 1)
    coef, parts = tables()

    def body(right_side, geometry, shift, node_order, elem_counts, share_lists):
        vmem = pl.BlockSpec(memory_space=pltpu.VMEM)
        hbm = pl.BlockSpec(memory_space=pltpu.HBM)
        plane = jax.ShapeDtypeStruct((ROWS, LANES), jnp.float32)

        def stay(x):
            return pltpu.with_memory_space_constraint(x, pltpu.HBM)

        vector = pltpu.VMEM((PAD, LANES), jnp.float32)
        solved, left = pl.pallas_call(
            functools.partial(kernel, n_px, n_py),
            out_shape=(plane, plane),
            in_specs=[hbm] * 4 + [vmem] + [hbm] * 3,
            out_specs=(vmem, vmem),
            scratch_shapes=[
                pltpu.VMEM((1, ROWS * LANES), jnp.float32),
                pltpu.VMEM((3, ELEMS, 4 * LANES), jnp.float32),
                pltpu.VMEM((1, ELEMS), jnp.float32),
                pltpu.VMEM((ELEMS, 4 * LANES), jnp.int32),
                pltpu.VMEM((4, FACE + 2 * DIAG), jnp.int32),
                pltpu.VMEM(coef.shape, jnp.float32),
                pltpu.VMEM(parts.shape, jnp.bfloat16),
                pltpu.VMEM((ELEMS, LANES), jnp.float32),
                vector,
                vector,
                vector,
                vector,
                pltpu.VMEM((8 * ELEMS + 8, LANES), jnp.float32),
                pltpu.VMEM((8 * ELEMS + 8, LANES), jnp.float32),
                pltpu.VMEM((3, PAD, LANES), jnp.float32),
                pltpu.VMEM((8 * ELEMS + 8, LANES), jnp.int32),
                pltpu.VMEM((80, LANES), jnp.int32),
                pltpu.VMEM((8, LANES), jnp.int32),
                pltpu.VMEM((8, LANES), jnp.int32),
                vector,
                pltpu.VMEM((8, LANES), jnp.float32),
                pltpu.VMEM((8 * FACE_ROWS, LANES), jnp.float32),
                pltpu.VMEM((4 * FACE_ROWS + 8, LANES), jnp.int32),
                pltpu.VMEM((4 * FACE_ROWS, LANES), jnp.int32),
                pltpu.VMEM((8, 4 * LANES), jnp.int32),
                pltpu.VMEM((3 * TURN, LANES), jnp.float32),
                pltpu.VMEM((3 * TURN, LANES), jnp.float32),
                pltpu.VMEM((3 * 32, LANES), jnp.float32),
                pltpu.VMEM((n_px + n_py, 1, LANES), jnp.float32),
                pltpu.SemaphoreType.DMA((count,)),
                pltpu.SemaphoreType.DMA((count,)),
                pltpu.SemaphoreType.DMA((7,)),
            ],
            compiler_params=pltpu.CompilerParams(
                collective_id=0, has_side_effects=True, vmem_limit_bytes=32 * 2**20
            ),
            cost_estimate=pl.CostEstimate(
                flops=10**8, bytes_accessed=2 * 10**6, transcendentals=0
            ),
        )(
            stay(right_side[0]),
            stay(geometry[0, 0]),
            stay(shift[0]),
            stay(node_order[0, 0]),
            elem_counts,
            stay(share_lists[0, 0]),
            stay(jnp.asarray(coef)),
            stay(jnp.asarray(parts)),
        )
        shape = (1, 1, ROWS * LANES)
        return solved.reshape(shape), left.reshape(shape)

    return jax.shard_map(
        body,
        mesh=mesh,
        in_specs=(
            P("px", "py", None),
            P("px", "py", None, None, None),
            P("px", "py", None),
            P("px", "py", None, None),
            P("px", "py"),
            P("px", "py", None, None),
        ),
        out_specs=(P("px", "py", None), P("px", "py", None)),
        check_vma=False,
    )
```

```python
import functools

import jax
import jax.numpy as jnp
import numpy as np
from jax import lax
from jax.experimental import pallas as pl
from jax.experimental.pallas import tpu as pltpu
from jax.sharding import PartitionSpec as P

STRIDE = 344
FACE = 1280
DIAG = 128
ELEMS = 48
LANES = 128
ROWS = 129
PAD = 136
FACE_ROWS = FACE // LANES
TURN = 80
SCALE = 2.0**-16
ROW_OF = [e * STRIDE // LANES for e in range(ELEMS)]
LOWER = (1, 3, 2, 3)
UPPER = (0, 2, 0, 1)
FACE_STEPS = ((1, 0), (-1, 0), (0, 1), (0, -1))
DIAG_STEPS = ((1, 1), (1, -1), (-1, 1), (-1, -1))
DIAG_LIST = (0, 0, 1, 1)


def gll_derivative():
    degree = 7
    points = np.array(
        [
            -1.0,
            -0.8717401485096066,
            -0.5917001814331423,
            -0.2092992179024789,
            0.2092992179024789,
            0.5917001814331423,
            0.8717401485096066,
            1.0,
        ]
    )
    before = np.ones(8)
    current = points * 1.0
    for order in range(1, degree):
        following = ((2 * order + 1) * points * current - order * before) / (order + 1)
        before = current
        current = following
    same = np.arange(8)[:, None] == np.arange(8)[None, :]
    spacing = np.where(same, 1.0, points[:, None] - points[None, :])
    matrix = np.where(same, 0.0, current[:, None] / (current[None, :] * spacing))
    corner = np.array([-14.0, 0.0, 0.0, 0.0, 0.0, 0.0, 0.0, 14.0])
    return matrix + np.where(same, corner[:, None], 0.0)


def tables():
    deriv = gll_derivative()
    half = np.arange(LANES) // 64

    def lanes_of(matrix):
        rows = []
        for out in range(4):
            for src in range(4):
                rows.append(matrix[2 * out + half, 2 * src + half])
                rows.append(matrix[2 * out + half, 2 * src + 1 - half])
        return np.stack(rows)

    coef = np.concatenate([lanes_of(deriv), SCALE * lanes_of(deriv.T)])
    second = np.kron(np.eye(2), np.kron(deriv, np.eye(8)))
    third = np.kron(np.eye(16), deriv)
    ahead = np.concatenate([second.T, third.T], axis=1)
    back = SCALE * np.concatenate([second, third], axis=0)
    halves = [ahead[:, :LANES], ahead[:, LANES:], back]
    parts = np.concatenate([part for half in halves for part in three_parts(half)], axis=0)
    return np.asarray(coef, np.float32), parts


def three_parts(table):
    rest = np.asarray(table, np.float32)
    parts = []
    for _ in range(3):
        part = rest.astype(jnp.bfloat16)
        parts.append(part)
        rest = rest - part.astype(np.float32)
    return parts


def three_ways(values):
    first = values.astype(jnp.bfloat16)
    rest = values - first.astype(jnp.float32)
    second = rest.astype(jnp.bfloat16)
    return first, second, (rest - second.astype(jnp.float32)).astype(jnp.bfloat16)


def product(pieces, table):
    left = jnp.concatenate(pieces, axis=1)
    return jnp.dot(left, table, preferred_element_type=jnp.float32)


def take_lanes(values, lanes):
    return jnp.take_along_axis(values, lanes, axis=1, mode="promise_in_bounds")


def pick(sources, index):
    high = index >> 7
    lanes = index & 127
    total = None
    for j, source in enumerate(sources):
        found = take_lanes(source, lanes)
        total = jnp.where(high == j, found, 0.0 if total is None else total)
    return total


def sum_exactly(rows):
    errors = []
    while len(rows) > 1:
        sums_of = []
        for x, y in zip(rows[::2], rows[1::2]):
            total = x + y
            part = total - x
            errors.append((x - (total - part)) + (y - part))
            sums_of.append(total)
        rows = sums_of
    while len(errors) > 1:
        odd = errors[len(errors) // 2 * 2 :]
        errors = [x + y for x, y in zip(errors[::2], errors[1::2])] + odd
    return rows[0], errors[0]


def split(x):
    small = x * 2.0**-16
    wide = small * 4097.0
    high = (wide - (wide - small)) * 2.0**16
    return high, x - high


def product_less(factor, times, less):
    product = factor * times[0]
    (f_high, f_low), (t_high, t_low) = split(factor), split(times[0])
    error = ((f_high * t_high - product) + f_high * t_low + f_low * t_high) + f_low * t_low
    return (product - less[0]) + ((error - less[1]) + factor * times[1])


def eight(row):
    return jnp.broadcast_to(row, (8, row.shape[1]))


def iota(shape, dim):
    return lax.broadcasted_iota(jnp.int32, shape, dim)


def as_bf16(values):
    return values.astype(jnp.float32).astype(jnp.bfloat16)


def one_hot_lanes(low, row_number):
    low = as_bf16(low)
    one = jnp.ones((LANES, LANES), jnp.bfloat16)
    zero = jnp.zeros((LANES, LANES), jnp.bfloat16)
    return jnp.concatenate(
        [
            jnp.where(row_number == low[:, at : at + LANES], one, zero)
            for at in range(0, low.shape[1], LANES)
        ],
        axis=1,
    )


def over_lanes(left, right):
    return lax.dot_general(
        left, right, (((1,), (1,)), ((), ())), preferred_element_type=jnp.float32
    )


def inverse_rows(high, low, groups, row_number):
    count = high.shape[1]
    number = iota((groups, count), 1) + 1
    hit = high == iota((groups, count), 0)
    tens = jnp.where(hit, number >> 4, 0).astype(jnp.float32)
    ones = jnp.where(hit, number & 15, 0).astype(jnp.float32)
    left = jnp.concatenate([tens, ones], axis=0).astype(jnp.bfloat16)
    found = over_lanes(left, one_hot_lanes(low, row_number))
    return (16.0 * found[:groups] + found[groups:]).astype(jnp.int32) - 1


def kernel(
    n_px,
    n_py,
    rhs_hbm,
    geo_hbm,
    shift_hbm,
    order_hbm,
    count_ref,
    lists_hbm,
    coef_hbm,
    parts_hbm,
    sol_ref,
    res_ref,
    rhs_ref,
    geo_ref,
    shift_ref,
    order_ref,
    lists_ref,
    coef_ref,
    parts_ref,
    factors,
    resid,
    image,
    second,
    part,
    windows,
    spread,
    sums,
    elem_inv,
    face_inv,
    cross_inv,
    wrap_inv,
    inv_mult,
    cross_src,
    stack,
    list_idx,
    inv_idx,
    wrap_idx,
    send,
    recv,
    recv_diag,
    red,
    send_sem,
    recv_sem,
    load_sem,
):
    loads = {}
    for number, (name, src, dst) in enumerate(
        (
            ("lists", lists_hbm, lists_ref),
            ("rhs", rhs_hbm, rhs_ref),
            ("order", order_hbm, order_ref),
            ("shift", shift_hbm, shift_ref),
            ("parts", parts_hbm, parts_ref),
            ("geo", geo_hbm, geo_ref),
            ("coef", coef_hbm, coef_ref),
        )
    ):
        loads[name] = pltpu.make_async_copy(src, dst, load_sem.at[number])
        loads[name].start()

    px = lax.axis_index("px")
    py = lax.axis_index("py")

    def moved(step_x, step_y):
        return (lax.rem(px + step_x + n_px, n_px), lax.rem(py + step_y + n_py, n_py))

    sizes = (n_px, n_py)

    def place(stage):
        return px if stage == 0 else py

    def far_first(size):
        return sorted(range(1, size), key=lambda d: (-min(d, size - d), d))

    def partners(stage):
        if stage == 0:
            return [(lax.rem(px + d, n_px), py) for d in far_first(n_px)]
        return [(px, lax.rem(py + d, n_py)) for d in far_first(n_py)]

    everyone = [moved(*step) for step in FACE_STEPS + DIAG_STEPS]
    everyone += partners(0) + partners(1)
    barrier = pltpu.get_barrier_semaphore()
    for other in everyone:
        pl.semaphore_signal(
            barrier, inc=1, device_id=other, device_id_type=pl.DeviceIdType.MESH
        )

    copies = []

    def start_copy(src, dst, other):
        number = len(copies)
        copy = pltpu.make_async_remote_copy(
            src_ref=src,
            dst_ref=dst,
            send_sem=send_sem.at[number],
            recv_sem=recv_sem.at[number],
            device_id=other,
            device_id_type=pl.DeviceIdType.MESH,
        )
        copy.start()
        copies.append(copy)
        return copy

    def start_exchange(turn):
        started = []
        for f, step in enumerate(FACE_STEPS):
            started.append(
                start_copy(
                    send.at[pl.ds(TURN * turn + 16 * f, 16)],
                    recv.at[pl.ds(TURN * turn + 16 * (f ^ 1), 16)],
                    moved(*step),
                )
            )
        for d, step in enumerate(DIAG_STEPS):
            started.append(
                start_copy(
                    send.at[pl.ds(TURN * turn + 16 * DIAG_LIST[d] + 8, 8)],
                    recv_diag.at[pl.ds(32 * turn + 8 * (3 - d), 8)],
                    moved(*step),
                )
            )
        return started

    def start_sum(stage, row):
        mine = stage * n_px + place(stage)
        red[pl.ds(mine, 1)] = row[None]
        return [start_copy(red.at[mine], red.at[mine], other) for other in partners(stage)]

    def end_sum(stage, started):
        for copy in started:
            copy.wait_recv()
        return sum_exactly([red[stage * n_px + slot] for slot in range(sizes[stage])])

    live = count_ref[...]

    half = FACE_ROWS // 2

    def pair_up(target, at, upper, lower):
        target[at : at + 4, :] = upper
        target[at + 4 : at + 8, :] = lower

    def stack_rows(source, first, step):
        for j in range(FACE_ROWS):
            rows = source[pl.ds(first + j, 4, stride=step), :]
            pair_up(stack, 8 * j, rows, rows)
        return [stack[8 * j : 8 * j + 8, :] for j in range(FACE_ROWS)]

    def fill_send(turn, source):
        rows = stack_rows(source, 0, FACE_ROWS)
        for i in range(half):
            found = pick(rows, list_idx[8 * i : 8 * i + 8, :])
            send[pl.ds(TURN * turn + i, 4, stride=16), :] = found[0:4]
            send[pl.ds(TURN * turn + i + half, 4, stride=16), :] = found[4:8]
        first = 4 * FACE_ROWS
        for at, q in enumerate(LOWER + UPPER):
            cross_src[at : at + 1, :] = source[first + q : first + q + 1, :]
        found = pick([cross_src[...]], list_idx[8 * half : 8 * half + 8, :])
        send[pl.ds(TURN * turn + FACE_ROWS, 4, stride=16), :] = found[0:4]
        send[pl.ds(TURN * turn + FACE_ROWS + 1, 4, stride=16), :] = found[4:8]

    def add_received(turn, target):
        rows = stack_rows(recv, TURN * turn, 16)
        for i in range(half):
            found = pick(rows, inv_idx[8 * i : 8 * i + 8, :])
            target[pl.ds(i, 4, stride=FACE_ROWS), :] += found[0:4]
            target[pl.ds(i + half, 4, stride=FACE_ROWS), :] += found[4:8]
        for part in range(2):
            at = TURN * turn + FACE_ROWS + part
            cross_src[4 * part : 4 * part + 4, :] = recv[pl.ds(at, 4, stride=16), :]
        for row, q, i in ((2, 2, 2), (3, 3, 3), (6, 0, 2), (7, 1, 3)):
            at = 32 * turn + 8 * q + i
            cross_src[row : row + 1, :] += recv_diag[at : at + 1, :]
        found = pick([cross_src[...]], cross_inv[...])
        first = 4 * FACE_ROWS
        for at, q in enumerate(LOWER + UPPER):
            target[first + q : first + q + 1, :] += found[at : at + 1]

    element = iota((ELEMS, LANES), 0)
    offset = (element * STRIDE) & 127
    is_last = element == live - 1

    def orders(c):
        return order_ref[:, c * LANES : (c + 1) * LANES]

    def last_row(values):
        return jnp.sum(jnp.where(is_last, values, jnp.zeros_like(values)), axis=0, keepdims=True)

    def set_up():
        row_number = as_bf16(iota((LANES, LANES), 0))
        for f in range(4):
            row = lists_ref[f : f + 1, 0:FACE]
            face_inv[16 * f : 16 * f + 16, :] = inverse_rows(row >> 7, row & 127, 16, row_number)
            for part in range(2):
                at = FACE + part * DIAG
                row = lists_ref[f : f + 1, at : at + DIAG]
                number = (iota((8, DIAG), 1) + 1).astype(jnp.float32).astype(jnp.bfloat16)
                found = over_lanes(number, one_hot_lanes(row, row_number))
                cross_inv[4 * part + f : 4 * part + f + 1, :] = found[0:1].astype(jnp.int32) - 1
        for i in range(half):
            pair_up(
                inv_idx,
                8 * i,
                face_inv[pl.ds(i, 4, stride=16), :],
                face_inv[pl.ds(i + half, 4, stride=16), :],
            )
        inv_mult[...] = jnp.ones_like(inv_mult)
        for f in range(4):
            named = face_inv[16 * f : 16 * f + FACE_ROWS, :] >= 0
            inv_mult[f * FACE_ROWS : (f + 1) * FACE_ROWS, :] = jnp.where(named, 0.5, 1.0)
        for q in range(4):
            copies_of = jnp.ones((1, LANES), jnp.float32)
            for part, regions in enumerate((LOWER, UPPER)):
                for f, region in enumerate(regions):
                    if region == q:
                        row = cross_inv[4 * part + f : 4 * part + f + 1, :]
                        copies_of = copies_of + jnp.where(row >= 0, 1.5, 0.0)
            at = 4 * FACE_ROWS + q
            inv_mult[at : at + 1, :] = 1.0 / copies_of

        @pl.loop(0, ELEMS // 16)
        def _(group):
            block = order_ref[pl.ds(pl.multiple_of(16 * group, 16), 16), :]
            for s in range(16):
                e = 16 * group + s
                row = block[s : s + 1]
                shifted = row + s * STRIDE % LANES
                own = jnp.where(live <= e, 0, jnp.where(live == e + 1, STRIDE, 4 * LANES))
                high = jnp.where(row >= own, 7, shifted >> 7)
                elem_inv[pl.ds(pl.multiple_of(8 * e, 8), 8), :] = inverse_rows(
                    high, shifted & 127, 8, row_number
                )

        wrapped = jnp.concatenate([last_row(orders(c)) for c in range(4)], axis=1) - STRIDE
        wrap_inv[...] = inverse_rows(wrapped >> 7, wrapped & 127, 8, row_number)
        wrap_idx[...] = eight(wrapped)

    def derivative(chunks, first):
        swapped = [pltpu.roll(u, 64, 1) for u in chunks]
        result = []
        for out in range(4):
            total = None
            for src in range(4):
                at = first + (out * 4 + src) * 2
                term = coef_ref[at : at + 1, :] * chunks[src]
                total = term if total is None else total + term
                total = total + coef_ref[at + 1 : at + 2, :] * swapped[src]
            result.append(total)
        return result

    def stacked(k):
        return jnp.concatenate(
            [geo_ref[k, :, c * LANES : (c + 1) * LANES] for c in range(4)], axis=0
        )

    def operate(source):
        for e, row in enumerate(ROW_OF):
            windows[8 * e : 8 * e + 8, :] = source[row : row + 8, :]
        rows = [windows[pl.ds(k, ELEMS, stride=8), :] for k in range(5)]
        chunks = []
        for c in range(4):
            order = orders(c)
            around = pick(
                [eight(source[0:1, :]), eight(source[1:2, :])],
                wrap_idx[:, c * LANES : (c + 1) * LANES],
            )[0:1]
            values = pick(rows, order + offset)
            chunks.append(jnp.where(is_last & (order >= STRIDE), around, values))
        a1, a2, a3 = (
            jnp.concatenate(
                [parts_ref[at : at + LANES, :] for at in (k * LANES, (3 + k) * LANES)], axis=1
            )
            for k in range(3)
        )
        ahead = jnp.concatenate([a1, a1, a2, a2, a1, a3], axis=0)
        b1, b2, b3 = (
            parts_ref[(6 + 2 * k) * LANES : (8 + 2 * k) * LANES, :] for k in range(3)
        )
        back_wide = jnp.concatenate([b1, b2], axis=1)
        back_wide = jnp.concatenate([back_wide, back_wide], axis=0)
        back_rest = jnp.concatenate([b1, b3], axis=0)
        u1, u2, u3 = three_ways(jnp.concatenate(chunks, axis=0))
        grads = product([u1, u2, u1, u2, u3, u1], ahead)
        fluxes = jnp.concatenate(
            [stacked(1) * grads[:, :LANES], stacked(2) * grads[:, LANES:]], axis=1
        )
        u1, u2, u3 = three_ways(fluxes)
        wide = product([u1, u2], back_wide)
        terms = product([u3, u1], back_rest) + wide[:, LANES:] + wide[:, :LANES]
        grad = derivative(chunks, 0)
        grad = [geo_ref[0, :, c * LANES : (c + 1) * LANES] * grad[c] for c in range(4)]
        first = derivative(grad, 32)
        factor = factors[...]
        result = [
            terms[c * ELEMS : (c + 1) * ELEMS] + first[c] + factor * chunks[c] for c in range(4)
        ]
        for k in range(5):
            spread[pl.ds(k, ELEMS, stride=8), :] = pick(
                result, elem_inv[pl.ds(k, ELEMS, stride=8), :]
            )
        for e, row in enumerate(ROW_OF):
            sums[e % 3, row : row + 8, :] = spread[8 * e : 8 * e + 8, :]
        sums[0, 0:8, :] += pick([eight(last_row(r)) for r in result], wrap_inv[...])
        return sums[0] + sums[1] + sums[2]

    lane = iota((1, LANES), 1)

    def dots(first, row, *products):
        for k, product in enumerate(products, first):
            total = jnp.sum(jnp.sum(product, axis=0, keepdims=True), axis=1, keepdims=True)
            row = jnp.where(lane == k, total, row)
        return row

    send[...] = jnp.zeros_like(send)
    spread[...] = jnp.zeros_like(spread)
    sums[...] = jnp.zeros_like(sums)
    resid[...] = jnp.zeros_like(resid)
    loads["lists"].wait()
    loads["rhs"].wait()
    for i in range(half):
        pair_up(
            list_idx,
            8 * i,
            lists_ref[:, i * LANES : (i + 1) * LANES],
            lists_ref[:, (i + half) * LANES : (i + half + 1) * LANES],
        )
    pair_up(
        list_idx,
        8 * half,
        lists_ref[:, FACE : FACE + DIAG],
        lists_ref[:, FACE + DIAG : FACE + 2 * DIAG],
    )
    for i in range(ROWS):
        resid[i : i + 1, :] = rhs_ref[:, i * LANES : (i + 1) * LANES]
    slot = iota((ROWS, LANES), 0) * LANES + iota((ROWS, LANES), 1)
    resid[0:ROWS, :] = jnp.where(slot < live * STRIDE, resid[0:ROWS, :], 0.0)
    fill_send(0, resid)
    pl.semaphore_wait(barrier, len(everyone))
    exchange = start_exchange(0)
    loads["order"].wait()
    loads["shift"].wait()
    set_up()
    same = iota((ELEMS, ELEMS), 0) == iota((ELEMS, ELEMS), 1)
    column = jnp.sum(jnp.where(same, shift_ref[...], 0.0), axis=1, keepdims=True)
    factors[...] = jnp.broadcast_to(SCALE * column, (ELEMS, LANES))
    for name in ("parts", "geo", "coef"):
        loads[name].wait()
    for copy in exchange:
        copy.wait_recv()
    add_received(0, resid)

    part[...] = operate(resid)
    image[...] = part[...]
    fill_send(1, image)
    exchange = start_exchange(1)
    res0 = resid[...]
    row = jnp.zeros((1, LANES), jnp.float32)
    row = dots(0, row, res0 * res0 * inv_mult[...], res0 * part[...])
    for copy in exchange:
        copy.wait_recv()
    add_received(1, image)

    part[...] = operate(image)
    image0 = image[...]
    row = dots(2, row, image0 * image0 * inv_mult[...], image0 * part[...])
    summing = start_sum(0, row)
    second[...] = part[...]
    fill_send(2, second)
    exchange = start_exchange(2)
    total, rest = end_sum(0, summing)
    summing = start_sum(1, jnp.where(lane < 64, total, pltpu.roll(rest, 64, 1)))
    for copy in exchange:
        copy.wait_recv()
    add_received(2, second)
    for copy in copies[: -len(summing)]:
        copy.wait_send()
    total, rest = end_sum(1, summing)
    rest = rest + pltpu.roll(total, 64, 1)

    def scalar(k):
        return total[:, k : k + 1], rest[:, k : k + 1]

    norm0, energy0, square, bend = (scalar(k) for k in range(4))
    alpha0 = norm0[0] / energy0[0]
    lack = product_less(alpha0, energy0, norm0)
    excess = product_less(alpha0, square, energy0)
    curve = product_less(alpha0, bend, square)
    norm1 = alpha0 * excess - lack
    beta = norm1 / norm0[0]
    energy1 = (alpha0 * curve - excess) + beta * (beta * energy0[0] - 2.0 * excess)
    alpha1 = norm1 / energy1

    res0 = resid[...]
    image0 = image[...]
    res1 = res0 - alpha0 * image0
    image1 = (image0 - alpha0 * second[...]) + beta * image0
    solved = (SCALE * alpha0) * res0 + (SCALE * alpha1) * (res1 + beta * res0)
    left = res1 - alpha1 * image1
    for i in range(ROWS):
        sol_ref[:, i * LANES : (i + 1) * LANES] = solved[i : i + 1]
        res_ref[:, i * LANES : (i + 1) * LANES] = left[i : i + 1]
    for copy in summing:
        copy.wait_send()


def solution(mesh):
    n_px = mesh.shape["px"]
    n_py = mesh.shape["py"]
    count = 3 * 8 + (n_px - 1 + n_py - 1)
    coef, parts = tables()

    def body(right_side, geometry, shift, node_order, elem_counts, share_lists):
        vmem = pl.BlockSpec(memory_space=pltpu.VMEM)
        hbm = pl.BlockSpec(memory_space=pltpu.HBM)
        plane = jax.ShapeDtypeStruct((1, ROWS * LANES), jnp.float32)

        def stay(x):
            return pltpu.with_memory_space_constraint(x, pltpu.HBM)

        vector = pltpu.VMEM((PAD, LANES), jnp.float32)
        solved, left = pl.pallas_call(
            functools.partial(kernel, n_px, n_py),
            out_shape=(plane, plane),
            in_specs=[hbm] * 4 + [vmem] + [hbm] * 3,
            out_specs=(vmem, vmem),
            scratch_shapes=[
                pltpu.VMEM((1, ROWS * LANES), jnp.float32),
                pltpu.VMEM((3, ELEMS, 4 * LANES), jnp.float32),
                pltpu.VMEM((1, ELEMS), jnp.float32),
                pltpu.VMEM((ELEMS, 4 * LANES), jnp.int32),
                pltpu.VMEM((4, FACE + 2 * DIAG), jnp.int32),
                pltpu.VMEM(coef.shape, jnp.float32),
                pltpu.VMEM(parts.shape, jnp.bfloat16),
                pltpu.VMEM((ELEMS, LANES), jnp.float32),
                vector,
                vector,
                vector,
                vector,
                pltpu.VMEM((8 * ELEMS + 8, LANES), jnp.float32),
                pltpu.VMEM((8 * ELEMS + 8, LANES), jnp.float32),
                pltpu.VMEM((3, PAD, LANES), jnp.float32),
                pltpu.VMEM((8 * ELEMS + 8, LANES), jnp.int32),
                pltpu.VMEM((80, LANES), jnp.int32),
                pltpu.VMEM((8, LANES), jnp.int32),
                pltpu.VMEM((8, LANES), jnp.int32),
                vector,
                pltpu.VMEM((8, LANES), jnp.float32),
                pltpu.VMEM((8 * FACE_ROWS, LANES), jnp.float32),
                pltpu.VMEM((4 * FACE_ROWS + 8, LANES), jnp.int32),
                pltpu.VMEM((4 * FACE_ROWS, LANES), jnp.int32),
                pltpu.VMEM((8, 4 * LANES), jnp.int32),
                pltpu.VMEM((3 * TURN, LANES), jnp.float32),
                pltpu.VMEM((3 * TURN, LANES), jnp.float32),
                pltpu.VMEM((3 * 32, LANES), jnp.float32),
                pltpu.VMEM((n_px + n_py, 1, LANES), jnp.float32),
                pltpu.SemaphoreType.DMA((count,)),
                pltpu.SemaphoreType.DMA((count,)),
                pltpu.SemaphoreType.DMA((7,)),
            ],
            compiler_params=pltpu.CompilerParams(
                collective_id=0, has_side_effects=True, vmem_limit_bytes=32 * 2**20
            ),
            cost_estimate=pl.CostEstimate(
                flops=10**8, bytes_accessed=2 * 10**6, transcendentals=0
            ),
        )(
            stay(right_side[0]),
            stay(geometry[0, 0]),
            stay(shift[0]),
            stay(node_order[0, 0]),
            elem_counts,
            stay(share_lists[0, 0]),
            stay(jnp.asarray(coef)),
            stay(jnp.asarray(parts)),
        )
        shape = (1, 1, ROWS * LANES)
        return solved.reshape(shape), left.reshape(shape)

    return jax.shard_map(
        body,
        mesh=mesh,
        in_specs=(
            P("px", "py", None),
            P("px", "py", None, None, None),
            P("px", "py", None),
            P("px", "py", None, None),
            P("px", "py"),
            P("px", "py", None, None),
        ),
        out_specs=(P("px", "py", None), P("px", "py", None)),
        check_vma=False,
    )
```
